32 devices in a mesh: lon: 8 (over y, x, core), lat: 4 (over z).
Axes of the slice: x: 2, y: 2, z: 4, core: 2. Of those that a mesh axis runs over, the one named last changes fastest.
Arguments:
- volume_b: float32 [4, 40, 192, 1024], P(None, None, 'lat', 'lon'), may hold values from -6 to 6
- tokens_a: bfloat16 [8, 24, 128, 768], P(None, 'lat', 'lon'), may hold values from -6 to 6
- embed_weight: bfloat16 [4032, 768], P('lat'), may hold values from -0.09375 to 0.09375
- unembed_weight: bfloat16 [4032, 768], P('lat'), may hold values from -0.21875 to 0.21875
Outputs:
- tokens_b: bfloat16 [8, 24, 128, 768], P(None, 'lat', 'lon')
- volume_a: float32 [4, 40, 192, 1024], P(None, None, 'lat', 'lon')
The draws below stay inside these ranges and needn't reach their ends.
All inputs are finite; a program needn't handle non-finite values.
Results may differ from the reference program's by a relative error of at most 0.005.
Values may be sent and summed in bfloat16 or wider, within the bound.
No kernel may reach another device: no remote copies, remote signals or barrier semaphores. Data moves between devices by JAX's collectives and lax.ppermute only.
A program may use at most 704 MiB of HBM per device.

```python
import jax
import jax.numpy as jnp
from jax import lax

D = 768
VARS = 4
LEV_TOK = 8
LEVELS = 40
K = 4032
NI = 128
NJ = 24
NLON = 1024
NLAT = 192


def level_of(key, shape, pieces, least, largest):
    factor_of, own = 1.0, jax.random.fold_in(key, 6)
    for dim, shards_of in pieces:
        heights = jnp.exp(jax.random.uniform(jax.random.fold_in(own, dim), (shards_of,), jnp.float32, least / len(pieces), largest / len(pieces)))
        factor_of = factor_of * jnp.repeat(heights, shape[dim] // shards_of).reshape([-1 if axis == dim else 1 for axis in range(len(shape))])
    return factor_of


def noise(rng, dims, deviation, limit, split=(), kind=jnp.bfloat16):
    loudness = level_of(rng, dims, split, -0.22, 0.18) if split else 1.0
    entries = jax.random.normal(rng, dims, jnp.float32) * deviation * loudness
    return jnp.minimum(jnp.maximum(entries, -limit), limit).astype(kind)


def setup_inputs(seed: int = 0) -> dict:
    splits = jax.random.split(jax.random.key(seed), 5)
    volume_b = noise(splits[0], (VARS, LEVELS, NLAT, NLON), 1.0, 6.0, ((2, 4), (3, 8)), jnp.float32)
    tokens_a = noise(splits[1], (LEV_TOK, NJ, NI, D), 1.0, 6.0, ((1, 4), (2, 8)))
    embed_weight = noise(splits[2], (K, D), K ** -0.5, 0.09375, ((0, 4),))
    unembed_weight = noise(splits[3], (K, D), D ** -0.5, 0.21875, ((0, 4),))
    return dict(volume_b=volume_b, tokens_a=tokens_a, embed_weight=embed_weight, unembed_weight=unembed_weight)


def unfold_blocks(source, axis_at, blocks, stride, extent):
    dims_now = source.shape
    reshaped = source.reshape(dims_now[:axis_at] + (blocks + 1, stride) + dims_now[axis_at + 1:])
    leading = lax.slice_in_dim(reshaped, 0, blocks, axis=axis_at)
    trailing = lax.slice_in_dim(reshaped, 1, blocks + 1, axis=axis_at)
    trailing = lax.slice_in_dim(trailing, 0, extent - stride, axis=axis_at + 1)
    return jnp.concatenate([leading, trailing], axis=axis_at + 1)


def fold_blocks(source, axis_at, stride):
    extent = source.shape[axis_at + 1]
    primary = lax.slice_in_dim(source, 0, stride, axis=axis_at + 1)
    overflow = lax.slice_in_dim(source, stride, extent, axis=axis_at + 1)
    widths_main = [(0, 0)] * source.ndim
    widths_main[axis_at] = (0, 1)
    widths_over = [(0, 0)] * source.ndim
    widths_over[axis_at] = (1, 0)
    widths_over[axis_at + 1] = (0, 2 * stride - extent)
    summed = jnp.pad(primary, widths_main) + jnp.pad(overflow, widths_over)
    new_dims = source.shape[:axis_at] + (stride * (source.shape[axis_at] + 1),) + source.shape[axis_at + 2:]
    return summed.reshape(new_dims)


def reference(volume_b, tokens_a, embed_weight, unembed_weight):
    field = volume_b.astype(jnp.bfloat16)
    field = jnp.concatenate([field[..., NLON - 2:], field, field[..., :2]], axis=3)
    field = jnp.pad(field, ((0, 0), (1, 4), (2, 2), (0, 4)))

    def token_row(row_number):
        window = lax.dynamic_slice_in_dim(field, (row_number * 8).astype(jnp.int32), 12, 2)
        window = unfold_blocks(window, 1, LEV_TOK, 5, 7)
        window = unfold_blocks(window, 4, NI, 8, 12)
        window = window.transpose(1, 4, 0, 2, 3, 5).reshape(LEV_TOK * NI, K)
        product = jnp.dot(window, embed_weight, preferred_element_type=jnp.float32)
        return product.astype(jnp.bfloat16).reshape(LEV_TOK, NI, D)

    tokens_b = lax.map(token_row, jnp.arange(NJ, dtype=jnp.int32)).transpose(1, 0, 2, 3)

    def spread_row(trailing, row_number):
        chosen = lax.dynamic_index_in_dim(tokens_a, row_number, axis=1, keepdims=False)
        chosen = chosen.reshape(LEV_TOK * NI, D)
        patch = lax.dot_general(chosen, unembed_weight, (((1,), (1,)), ((), ())), preferred_element_type=jnp.float32)
        patch = patch.reshape(LEV_TOK, NI, VARS, 7, 12, 12).transpose(2, 0, 3, 4, 1, 5)
        patch = fold_blocks(patch, 4, 8)
        patch = fold_blocks(patch, 1, 5)
        patch = patch[:, 1:1 + LEVELS]
        centre = patch[..., 2:NLON + 2]
        centre = centre.at[..., 0:2].add(patch[..., NLON + 2:NLON + 4])
        centre = centre.at[..., NLON - 2:NLON].add(patch[..., 0:2])
        block_out = centre[:, :, 0:8] + jnp.pad(trailing, ((0, 0), (0, 0), (0, 4), (0, 0)))
        return centre[:, :, 8:12], block_out

    start_tail = jnp.zeros((VARS, LEVELS, 4, NLON), jnp.float32)
    last_tail, blocks = lax.scan(spread_row, start_tail, jnp.arange(NJ, dtype=jnp.int32))
    padded_rows = blocks.transpose(1, 2, 0, 3, 4).reshape(VARS, LEVELS, 8 * NJ, NLON)
    volume_a = jnp.concatenate([padded_rows[:, :, 2:], last_tail[:, :, 0:2]], axis=2)
    return tokens_b, volume_a
```

```python
import functools

import jax
import jax.numpy as jnp
from jax import lax
from jax.experimental import pallas as pl
from jax.experimental.pallas import tpu as pltpu
from jax.sharding import PartitionSpec as P

BF = jnp.bfloat16
F32 = jnp.float32
VMEM_LIMIT = 56 * 1024 * 1024
DZ, DY, DX = 7, 12, 12
SK, SY, SX = 5, 8, 8
GROUP = 8


def params():
    return pltpu.CompilerParams(vmem_limit_bytes=VMEM_LIMIT)


def spread_matrix(nk, ni, nx):
    rows = jnp.arange(nk * nx, dtype=jnp.int32)[:, None]
    cols = jnp.arange(DX * nk * ni, dtype=jnp.int32)[None, :]
    dx, k, i = cols // (nk * ni), cols // ni % nk, cols % ni
    return ((rows // nx == k) & (rows % nx == SX * i - 2 + dx)).astype(BF)


def edge_lanes(nv, nk):
    lane = jnp.arange(4 * nv * nk, dtype=jnp.int32)
    return lane // (2 * nv * nk), lane // (2 * nk) % nv, lane // nk % 2, lane % nk


def pick_matrix(nv, nk, nx):
    side, v, c, k = edge_lanes(nv, nk)
    rows = jnp.arange(nk * nx, dtype=jnp.int32)[None, :, None]
    x = jnp.where(side == 0, nx - 2 + c, c)
    own = jnp.arange(nv, dtype=jnp.int32)[:, None, None] == v
    return (own & (rows // nx == k) & (rows % nx == x)).astype(BF)


def edge_matrix(nv, nk, ni):
    side, v, c, k = (jnp.tile(a, 2)[None, :, None] for a in edge_lanes(nv, nk))
    half = (jnp.arange(8 * nv * nk, dtype=jnp.int32) // (4 * nv * nk))[None, :, None]
    cols = jnp.arange(4 * nk * ni, dtype=jnp.int32)[None, None, :]
    d, kk, i = cols // (nk * ni), cols // ni % nk, cols % ni
    own = jnp.arange(nv, dtype=jnp.int32)[:, None, None] == v
    left = (half == 0) & (side == 0) & (i == 0) & (d == c)
    right = (half == 1) & (side == 1) & (i == ni - 1) & (d == 2 + c)
    return (own & (k == kk) & (left | right)).astype(BF)


def out_edge_matrix(nk, ni):
    rows = jnp.arange(DX * nk * ni, dtype=jnp.int32)[:, None]
    lane = jnp.arange(128, dtype=jnp.int32)[None, :]
    dx, k, i = rows // (nk * ni), rows // ni % nk, rows % ni
    side, c, kk = lane // (2 * nk), lane // nk % 2, lane % nk
    left = (side == 0) & (i == 0) & (dx == c)
    right = (side == 1) & (i == ni - 1) & (dx == DX - 2 + c)
    return ((k == kk) & (left | right)).astype(BF)


def in_edge_matrix(nk, nx):
    row = jnp.arange(256, dtype=jnp.int32)[:, None]
    half, lane = row // 128, row % 128
    side, c, k = lane // (2 * nk), lane // nk % 2, lane % nk
    cols = jnp.arange(nk * nx, dtype=jnp.int32)[None, :]
    kk, x = cols // nx, cols % nx
    from_left = (half == 0) & (side == 1) & (x == c)
    from_right = (half == 1) & (side == 0) & (x == nx - 2 + c)
    return ((k == kk) & (from_left | from_right)).astype(BF)


def stack_levels(read, levels, nk, zeros, lhs, at, rows, dz):
    for k in range(nk):
        level = SK * k - 1 + dz
        block = read(level) if 0 <= level < levels else zeros
        lhs[at : at + rows, k * 128 : (k + 1) * 128] = block


def pack_kernel(nk, vol, pick, out, lhs, acc):
    v = pl.program_id(0)
    _, levels, ny, nx = vol.shape
    for dz in range(DZ):
        stack_levels(lambda l: vol[0, l].astype(BF), levels, nk, jnp.zeros((ny, nx), BF), lhs, dz * ny, ny, dz)
    part = jnp.dot(lhs[...], pick[0], preferred_element_type=F32)

    @pl.when(v == 0)
    def _():
        acc[...] = part

    @pl.when(v > 0)
    def _():
        acc[...] += part

    @pl.when(v == pl.num_programs(0) - 1)
    def _():
        out[...] = acc[...].astype(BF)


def im2col_kernel(nk, ni, nj, shard, vol, rim, edge, spread, edge_hot, out, lhs, q):
    _, levels, ny, nx = vol.shape
    main = DZ * ny
    for dz in range(DZ):
        stack_levels(lambda l: vol[0, l].astype(BF), levels, nk, jnp.zeros((ny, nx), BF), lhs, dz * ny, ny, dz)
    none = jnp.zeros((8, nx), F32)
    for k in range(nk):
        blocks = []
        for dz in range(DZ + 1):
            level = SK * k - 1 + dz
            blocks.append(rim[0, level] if 0 <= level < levels and dz < DZ else none)
        lhs[main : main + 64, k * 128 : (k + 1) * 128] = jnp.concatenate(blocks, axis=0).astype(BF)
    for pair in range(DX // 2):
        got = jnp.dot(lhs[...], spread[:, pair * 256 : (pair + 1) * 256], preferred_element_type=F32)
        if pair in (0, DX // 2 - 1):
            which = 0 if pair == 0 else 1
            got += jnp.dot(edge[...], edge_hot[0, :, which * 256 : (which + 1) * 256], preferred_element_type=F32)
        for h in range(2):
            dx = 2 * pair + h
            mine = got[:, h * 128 : (h + 1) * 128]
            for dz in range(DZ):
                q[dz, pl.ds(2 * DX + dx, ny, stride=DX), :] = mine[dz * ny : (dz + 1) * ny]
                at = main + 8 * dz
                q[dz, pl.ds(dx, 2, stride=DX), :] = mine[at : at + 2]
                q[dz, pl.ds(DX * (ny + 2) + dx, 2, stride=DX), :] = mine[at + 2 : at + 4]
    rows, padded, piece = shard
    head = piece * (GROUP - 1)
    per = SY * DX
    for j in range(nj):
        columns = jnp.concatenate([q[dz, per * j : per * j + DY * DX, :] for dz in range(DZ)], axis=0)
        gap = jnp.zeros((padded - rows, 128), F32)
        columns = jnp.concatenate([columns[:head], gap, columns[head:]], axis=0)
        out[0, j] = columns.T.astype(BF)


def weight_copies(gathered, sources, step, me, slot, sems):
    padded = slot.shape[0]
    piece = padded // GROUP
    if not gathered:
        (source,) = sources
        rows = source.shape[1]
        head = piece * (GROUP - 1)
        return [
            pltpu.make_async_copy(source.at[step, pl.ds(0, head)], slot.at[pl.ds(0, head)], sems.at[0]),
            pltpu.make_async_copy(source.at[step, pl.ds(rows - piece, piece)], slot.at[pl.ds(head, piece)], sems.at[1]),
        ]
    core = lax.rem(me, 2)
    a, b = 2 + 2 * core, 4 - 2 * core
    distances = ((0, a), (b, 6), (1, 1 + b), (1 + a, 7))
    copies = []
    for n, (source, pair) in enumerate(zip(sources, distances)):
        for h, distance in enumerate(pair):
            place = pl.multiple_of(lax.bitwise_xor(me, jnp.int32(distance)) * piece, piece)
            copies.append(
                pltpu.make_async_copy(source.at[h, step], slot.at[pl.ds(place, piece)], sems.at[2 * n + h])
            )
    return copies


def embed_kernel(n, gathered, first, last, vid, me, a, *refs):
    n_w = 4 if gathered else 1
    sources, refs = refs[:n_w], refs[n_w:]
    if not first:
        prev, refs = refs[0], refs[1:]
    out, a_buf, w_buf, acc, a_sem, w_sem = refs

    def copies(s):
        slot = s % 2
        return [pltpu.make_async_copy(a.at[vid[s]], a_buf.at[slot], a_sem.at[slot])] + weight_copies(
            gathered, sources, s, me[0], w_buf.at[slot], w_sem.at[slot]
        )

    for c in copies(0):
        c.start()
    total = None
    for s in range(n):
        if s + 1 < n:
            for c in copies(s + 1):
                c.start()
        for c in copies(s):
            c.wait()
        got = jnp.dot(a_buf[s % 2], w_buf[s % 2], preferred_element_type=F32)
        if s > 0:
            got += acc[...]
        elif not first:
            got += prev[...]
        if s < n - 1:
            acc[...] = got
        elif last:
            nk, nj, ni, width = out.shape
            for j in range(nj):
                out[:, j] = got[j * nk * ni : (j + 1) * nk * ni].astype(BF).reshape(nk, ni, width)
        else:
            out[...] = got


def unembed_kernel(gathered, first, vid, me, tokens, spread, out_hot, *refs):
    n_w = 4 if gathered else 1
    sources, refs = refs[:n_w], refs[n_w:]
    if not first:
        edge_before, refs = refs[0], refs[3:]
    vol, rim, edge, w_buf, t, r, q, lhs, rim_q, w_sem = refs
    s, n = pl.program_id(0), pl.num_programs(0)
    nk, nj, ni, _ = tokens.shape
    _, levels, ny, nx = vol.shape
    main, per, over, block = DZ * ny, SY * DX, (DY - SY) * DX, DY * DX
    padded = w_buf.shape[1]
    head, gap = padded // GROUP * (GROUP - 1), padded - DZ * block

    def copies(step):
        slot = lax.rem(step, 2)
        return weight_copies(gathered, sources, step, me[0], w_buf.at[slot], w_sem.at[slot])

    @pl.when(s == 0)
    def _():
        for c in copies(s):
            c.start()
        for j in range(nj):
            for k in range(nk):
                t[(j * nk + k) * ni : (j * nk + k + 1) * ni, :] = tokens[k, j]
        rim_q[...] = jnp.zeros_like(rim_q)
        if first:
            edge[...] = jnp.zeros_like(edge)
        else:
            edge[...] = edge_before[...]

    @pl.when(s + 1 < n)
    def _():
        for c in copies(s + 1):
            c.start()

    for c in copies(s):
        c.wait()
    r[...] = lax.dot_general(w_buf[lax.rem(s, 2)], t[...], (((1,), (1,)), ((), ())), preferred_element_type=F32)

    def rows_of(dz, j, start, stop):
        lanes = slice(j * 128, (j + 1) * 128)
        lo, hi = dz * block + start, dz * block + stop
        if hi <= head:
            return r[lo:hi, lanes]
        if lo >= head:
            return r[lo + gap : hi + gap, lanes]
        return jnp.concatenate([r[lo:head, lanes], r[head + gap : hi + gap, lanes]], axis=0)

    for dz in range(DZ):
        for j in range(nj + 1):
            if j == nj:
                q[dz, per * j : per * j + over, :] = rows_of(dz, j - 1, per, block)
            else:
                lead = rows_of(dz, j, 0, over)
                if j > 0:
                    lead += rows_of(dz, j - 1, per, block)
                q[dz, per * j : per * j + over, :] = lead
                q[dz, per * j + over : per * (j + 1), :] = rows_of(dz, j, over, per)
    for dx in range(DX):
        lanes = slice(dx * 128, (dx + 1) * 128)
        for dz in range(DZ):
            lhs[dz * ny : (dz + 1) * ny, lanes] = q[dz, pl.ds(2 * DX + dx, ny, stride=DX), :].astype(BF)
            rim_q[8 * dz : 8 * dz + 2, lanes] = q[dz, pl.ds(dx, 2, stride=DX), :]
            rim_q[8 * dz + 2 : 8 * dz + 4, lanes] = q[dz, pl.ds(DX * (ny + 2) + dx, 2, stride=DX), :]
    lhs[main : main + 64, :] = rim_q[...].astype(BF)
    side = jnp.dot(lhs[...], out_hot[...], preferred_element_type=F32)
    edge[...] += pltpu.roll(side, vid[s] * 32, 1)

    carry = None
    for pair in range(nk // 2):
        got = lax.dot_general(
            lhs[...], spread[pair * 256 : (pair + 1) * 256, :], (((1,), (1,)), ((), ())), preferred_element_type=F32
        )
        for h in range(2):
            k = 2 * pair + h
            mine = got[:, h * 128 : (h + 1) * 128]
            for dz in range(DZ):
                level = SK * k - 1 + dz
                here = mine[dz * ny : (dz + 1) * ny]
                beside = mine[main + 8 * dz : main + 8 * (dz + 1)]
                if dz < DZ - SK and k > 0:
                    here, beside = here + carry[dz][0], beside + carry[dz][1]
                if 0 <= level < levels and (dz < SK or k == nk - 1):
                    vol[0, level], rim[0, level] = here, beside
            carry = [
                (mine[dz * ny : (dz + 1) * ny], mine[main + 8 * dz : main + 8 * (dz + 1)]) for dz in range(SK, DZ)
            ]


def add_edges(edge, at, rows, hot, levels, nk, v, apply):
    mine = edge[at : at + rows * (DZ + (rows == 8)), :].astype(F32)
    width = mine.shape[1] // 2
    shift = lax.rem(128 - 32 * v, 128)
    mine = jnp.concatenate([pltpu.roll(mine[:, :width], shift, 1), pltpu.roll(mine[:, width:], shift, 1)], axis=1)
    mine = mine.astype(BF)
    carry = None
    for pair in range(nk // 2):
        got = jnp.dot(mine, hot[:, pair * 256 : (pair + 1) * 256], preferred_element_type=F32)
        for h in range(2):
            k = 2 * pair + h
            part = got[:, h * 128 : (h + 1) * 128]
            for dz in range(DZ):
                level = SK * k - 1 + dz
                here = part[dz * rows : (dz + 1) * rows]
                if dz < DZ - SK and k > 0:
                    here = here + carry[dz]
                if 0 <= level < levels and (dz < SK or k == nk - 1):
                    apply(level, here)
            carry = [part[dz * rows : (dz + 1) * rows] for dz in range(SK, DZ)]


def rim_kernel(nk, rim, edge, hot, out):
    _, levels, _, _ = rim.shape
    main = edge.shape[0] - 64

    def apply(level, here):
        out[0, level] = rim[0, level] + here

    add_edges(edge, main, 8, hot, levels, nk, pl.program_id(0), apply)


def close_kernel(nk, vol, edge, hot, beside, out):
    _, levels, ny, _ = vol.shape
    row = lax.broadcasted_iota(jnp.int32, (8, 128), 0)

    def apply(level, here):
        got = vol[0, level] + here
        lat = beside[0, level]
        out[0, level, 0:8] = got[0:8] + jnp.where(row < 2, lat, 0.0)
        out[0, level, 8 : ny - 8] = got[8 : ny - 8]
        out[0, level, ny - 8 : ny] = got[ny - 8 : ny] + jnp.where(row >= 6, lat, 0.0)

    add_edges(edge, 0, ny, hot, levels, nk, pl.program_id(0), apply)


def whole(shape):
    return pl.BlockSpec(shape, lambda *_: (0,) * len(shape))


def lead(shape):
    return pl.BlockSpec((1,) + tuple(shape[1:]), lambda v, *_: (v,) + (0,) * (len(shape) - 1))


ANY = pl.BlockSpec(memory_space=pl.ANY)


def cost(flops, bytes_accessed):
    return pl.CostEstimate(flops=int(flops), bytes_accessed=int(bytes_accessed), transcendentals=0)


def pack_edges(volume, nk):
    nv, levels, ny, nx = volume.shape
    pick = pick_matrix(nv, nk, nx)
    return pl.pallas_call(
        functools.partial(pack_kernel, nk),
        grid=(nv,),
        in_specs=[lead(volume.shape), lead(pick.shape)],
        out_specs=whole((DZ * ny, 128)),
        out_shape=jax.ShapeDtypeStruct((DZ * ny, 128), BF),
        scratch_shapes=[pltpu.VMEM((DZ * ny, nk * nx), BF), pltpu.VMEM((DZ * ny, 128), F32)],
        compiler_params=params(),
        cost_estimate=cost(2 * nv * DZ * ny * nk * nx * 256, volume.size * 4),
        name="pack_edges",
    )(volume, pick)


def im2col(volume, rim, edge, spread, dims):
    nk, nj, ni, padded = dims
    nv, levels, ny, nx = volume.shape
    hot = edge_matrix(nv, nk, ni)
    rows = DZ * ny + 64
    shape = (nv, nj, nk * ni, padded)
    return pl.pallas_call(
        functools.partial(im2col_kernel, nk, ni, nj, (DZ * DY * DX, padded, padded // GROUP)),
        grid=(nv,),
        in_specs=[lead(volume.shape), lead(rim.shape), whole(edge.shape), whole(spread.shape), lead(hot.shape)],
        out_specs=lead(shape),
        out_shape=jax.ShapeDtypeStruct(shape, BF),
        scratch_shapes=[pltpu.VMEM((rows, nk * nx), BF), pltpu.VMEM((DZ, DX * (ny + 4), 128), F32)],
        compiler_params=params(),
        cost_estimate=cost(3 * nv * rows * nk * nx * DX * 128, volume.size * 4 + 2 * nv * nj * 128 * padded),
        name="im2col",
    )(volume, rim, edge, spread, hot)


def embed(a, weights, vid, me, prev, gathered, last, token_shape):
    n = vid.shape[0]
    nv, rows, padded = a.shape
    width = weights[0].shape[-1]
    first = prev is None
    out_shape = jax.ShapeDtypeStruct(token_shape, BF) if last else jax.ShapeDtypeStruct((rows, width), F32)
    smem = pl.BlockSpec(memory_space=pltpu.SMEM)
    vmem = pl.BlockSpec(memory_space=pltpu.VMEM)
    return pl.pallas_call(
        functools.partial(embed_kernel, n, gathered, first, last),
        in_specs=[smem, smem, ANY] + [ANY] * len(weights) + ([] if first else [vmem]),
        out_specs=vmem,
        out_shape=out_shape,
        scratch_shapes=[
            pltpu.VMEM((2, rows, padded), BF),
            pltpu.VMEM((2, padded, width), BF),
            pltpu.VMEM((rows, width) if n > 1 else (8, 128), F32),
            pltpu.SemaphoreType.DMA((2,)),
            pltpu.SemaphoreType.DMA((2, GROUP)),
        ],
        compiler_params=params(),
        cost_estimate=cost(2 * n * rows * padded * width, 2 * n * padded * (rows + width) + 4 * rows * width),
        name="embed",
    )(vid, me, a, *weights, *([] if first else [prev]))


def unembed(tokens, weights, vid, me, spread, out_hot, prev, gathered, volume_shape, padded):
    n = vid.shape[0]
    nk, nj, ni, width = tokens.shape
    nv, levels, ny, nx = volume_shape
    first = prev is None
    rows = DZ * ny + 64
    out_shape = (
        jax.ShapeDtypeStruct(volume_shape, F32),
        jax.ShapeDtypeStruct((nv, levels, 8, nx), F32),
        jax.ShapeDtypeStruct((rows, 128), F32),
    )

    def chosen(shape):
        return pl.BlockSpec((1,) + tuple(shape[1:]), lambda s, vid, me: (vid[s],) + (0,) * (len(shape) - 1))

    n_in = 5 + len(weights)
    before = () if first else (prev[2], prev[0], prev[1])
    return pl.pallas_call(
        functools.partial(unembed_kernel, gathered, first),
        grid_spec=pltpu.PrefetchScalarGridSpec(
            num_scalar_prefetch=2,
            grid=(n,),
            in_specs=[whole(tokens.shape), whole(spread.shape), whole(out_hot.shape)]
            + [ANY] * len(weights)
            + ([] if first else [whole((rows, 128)), ANY, ANY]),
            out_specs=(chosen(volume_shape), chosen((nv, levels, 8, nx)), whole((rows, 128))),
            scratch_shapes=[
                pltpu.VMEM((2, padded, width), BF),
                pltpu.VMEM((nj * nk * ni, width), BF),
                pltpu.VMEM((padded, nj * nk * ni), F32),
                pltpu.VMEM((DZ, DX * (ny + 4), 128), F32),
                pltpu.VMEM((rows, DX * nk * ni), BF),
                pltpu.VMEM((64, DX * nk * ni), F32),
                pltpu.SemaphoreType.DMA((2, GROUP)),
            ],
        ),
        out_shape=out_shape,
        input_output_aliases={} if first else {n_in + 1: 0, n_in + 2: 1},
        compiler_params=params(),
        cost_estimate=cost(6 * n * padded * width * nj * 128, 2 * n * padded * width + 4 * n * levels * ny * nx),
        name="unembed",
    )(vid, me, tokens, spread, out_hot, *weights, *before)


def rim_sums(rim, edge, hot, nk):
    return pl.pallas_call(
        functools.partial(rim_kernel, nk),
        grid=(rim.shape[0],),
        in_specs=[lead(rim.shape), whole(edge.shape), whole(hot.shape)],
        out_specs=lead(rim.shape),
        out_shape=jax.ShapeDtypeStruct(rim.shape, F32),
        compiler_params=params(),
        cost_estimate=cost(1e8, 8 * rim.size),
        name="rim_sums",
    )(rim, edge, hot)


def close_volume(vol, edge, hot, beside, nk):
    return pl.pallas_call(
        functools.partial(close_kernel, nk),
        grid=(vol.shape[0],),
        in_specs=[lead(vol.shape), whole(edge.shape), whole(hot.shape), lead(beside.shape)],
        out_specs=lead(vol.shape),
        out_shape=jax.ShapeDtypeStruct(vol.shape, F32),
        compiler_params=params(),
        cost_estimate=cost(1e9, 8 * vol.size),
        name="close_volume",
    )(vol, edge, hot, beside)


def both_ways(up_rows, down_rows, axis, wrap):
    size = lax.axis_size(axis)
    up = [(i, (i + 1) % size) for i in range(size if wrap else size - 1)]
    return lax.ppermute(up_rows, axis, up), lax.ppermute(down_rows, axis, [(j, i) for i, j in up])


def piece_rows(rows):
    return -(-rows // (16 * GROUP)) * 16


def gather_rows(weight, me):
    rows, piece = weight.shape[0], piece_rows(weight.shape[0])
    size, devices = lax.axis_size("lat"), lax.axis_size("lon")
    own = lax.dynamic_slice_in_dim(weight, jnp.minimum(me * piece, rows - piece), piece, 0)
    got = [lax.ppermute(own, "lat", [(i, (i + s) % size) for i in range(size)]) for s in range(1, size)]
    near = jnp.stack(got)
    first = [(i, i ^ (2 + 2 * (i & 1))) for i in range(devices)]
    second = [(i, i ^ (4 - 2 * (i & 1))) for i in range(devices)]
    partner = [(i, i ^ 1) for i in range(devices)]
    pair = jnp.stack([near, lax.ppermute(near, "lon", first)])
    rest = lax.ppermute(pair, "lon", second)
    return pair, rest, lax.ppermute(pair, "lon", partner), lax.ppermute(rest, "lon", partner)


def per_device(volume_b, tokens_a, embed_weight, unembed_weight):
    nk, nj, ni, width = tokens_a.shape
    nv, levels, ny, nx = volume_b.shape
    rows = DZ * DY * DX
    padded = piece_rows(rows) * GROUP
    main = DZ * ny
    lat, lats = lax.axis_index("lat"), lax.axis_size("lat")
    me = lax.rem(lax.axis_index("lon"), GROUP).astype(jnp.int32)
    me1 = me.reshape(1)
    fast = embed_weight.shape[0] == rows and lax.axis_size("lon") % GROUP == 0
    spread = spread_matrix(nk, ni, nx)
    out_hot = out_edge_matrix(nk, ni)
    in_hot = in_edge_matrix(nk, nx)

    if fast:
        unembed_rest = gather_rows(unembed_weight, me)
        embed_rest = gather_rows(embed_weight, me)

    packed = pack_edges(volume_b, nk)
    from_left, from_right = both_ways(packed, packed, "lon", True)

    def lat_rows(at):
        voxels = volume_b[:, :, at : at + 2].astype(BF).reshape(-1, nx)
        corners = [a.reshape(DZ, ny, 128)[:, at : at + 2].reshape(-1, 128) for a in (from_left, from_right)]
        return jnp.concatenate([voxels] + corners, axis=0)

    above, below = both_ways(lat_rows(ny - 2), lat_rows(0), "lat", False)
    n_vox = nv * levels * 2

    def split(got):
        voxels = got[:n_vox].reshape(nv, levels, 2, nx)
        corners = got[n_vox:].reshape(2, DZ, 2, 128)
        return voxels, jnp.concatenate([corners[0], corners[1]], axis=-1)

    (vox_above, cor_above), (vox_below, cor_below) = split(above), split(below)
    rim = jnp.concatenate([vox_above, vox_below, jnp.zeros((nv, levels, 4, nx), BF)], axis=2).astype(F32)
    corners = jnp.concatenate([cor_above, cor_below, jnp.zeros((DZ, 4, 256), BF)], axis=1).reshape(8 * DZ, 256)
    edge = jnp.concatenate(
        [jnp.concatenate([from_left, from_right], axis=1), corners, jnp.zeros((64 - 8 * DZ, 256), BF)], axis=0
    )
    a = im2col(volume_b, rim, edge, spread, (nk, nj, ni, padded)).reshape(nv, nj * nk * ni, padded)

    if fast:
        own = lat.astype(jnp.int32).reshape(1)
        others = lax.rem(lat - jnp.arange(1, lats, dtype=jnp.int32) + lats, lats).astype(jnp.int32)
        part = unembed(
            tokens_a, (unembed_weight[None],), own, me1, spread, out_hot, None, False, volume_b.shape, padded
        )
        vol, vol_rim, vol_edge = unembed(
            tokens_a, unembed_rest, others, me1, spread, out_hot, part, True, volume_b.shape, padded
        )
        sums = embed(a, (embed_weight[None],), own, me1, None, False, False, tokens_a.shape)
        tokens_b = embed(a, embed_rest, others, me1, sums, True, True, tokens_a.shape)
    else:
        every = jnp.arange(nv, dtype=jnp.int32)
        weights = [
            lax.all_gather(w, "lat", axis=0, tiled=True).reshape(nv, rows, width)
            for w in (unembed_weight, embed_weight)
        ]
        vol, vol_rim, vol_edge = unembed(
            tokens_a, weights[:1], every, me1, spread, out_hot, None, False, volume_b.shape, padded
        )
        tokens_b = embed(a, weights[1:], every, me1, None, False, True, tokens_a.shape)

    sent = vol_edge.astype(BF)
    edges = jnp.concatenate(both_ways(sent, sent, "lon", True), axis=1)
    outer = rim_sums(vol_rim, edges, in_hot, nk)
    down, up = (outer[:, :, at : at + 2].astype(BF).reshape(-1, nx) for at in (0, 2))
    above, below = (x.reshape(nv, levels, 2, nx) for x in both_ways(up, down, "lat", False))
    beside = jnp.concatenate([above, jnp.zeros((nv, levels, 4, nx), BF), below], axis=2).astype(F32)
    volume_a = close_volume(vol, edges, in_hot, beside, nk)
    return tokens_b, volume_a


def solution(mesh):
    placed = (
        P(None, None, "lat", "lon"),
        P(None, "lat", "lon", None),
        P("lat", None),
        P("lat", None),
    )
    return jax.shard_map(
        per_device,
        mesh=mesh,
        in_specs=placed,
        out_specs=(P(None, "lat", "lon", None), P(None, None, "lat", "lon")),
        check_vma=False,
    )
```

```python
import functools

import jax
import jax.numpy as jnp
import numpy as np
from jax import lax
from jax.experimental import pallas as pl
from jax.experimental.pallas import tpu as pltpu
from jax.sharding import PartitionSpec as P

BF = jnp.bfloat16
F32 = jnp.float32
VMEM_LIMIT = 56 * 1024 * 1024
DZ, DY, DX = 7, 12, 12
SK, SY, SX = 5, 8, 8
GROUP = 8


def params():
    return pltpu.CompilerParams(vmem_limit_bytes=VMEM_LIMIT)


def spread_matrix(nk, ni, nx):
    rows = np.arange(nk * nx)[:, None]
    cols = np.arange(DX * nk * ni)[None, :]
    dx, k, i = cols // (nk * ni), cols // ni % nk, cols % ni
    return ((rows // nx == k) & (rows % nx == SX * i - 2 + dx)).astype(BF)


def edge_lanes(nv, nk):
    lane = np.arange(4 * nv * nk)
    return lane // (2 * nv * nk), lane // (2 * nk) % nv, lane // nk % 2, lane % nk


def pick_matrix(nv, nk, nx):
    side, v, c, k = edge_lanes(nv, nk)
    rows = np.arange(nk * nx)[None, :, None]
    x = np.where(side == 0, nx - 2 + c, c)
    own = np.arange(nv)[:, None, None] == v
    return (own & (rows // nx == k) & (rows % nx == x)).astype(BF)


def edge_matrix(nv, nk, ni):
    side, v, c, k = (np.tile(a, 2)[None, :, None] for a in edge_lanes(nv, nk))
    half = (np.arange(8 * nv * nk) // (4 * nv * nk))[None, :, None]
    cols = np.arange(4 * nk * ni)[None, None, :]
    d, kk, i = cols // (nk * ni), cols // ni % nk, cols % ni
    own = np.arange(nv)[:, None, None] == v
    left = (half == 0) & (side == 0) & (i == 0) & (d == c)
    right = (half == 1) & (side == 1) & (i == ni - 1) & (d == 2 + c)
    return (own & (k == kk) & (left | right)).astype(BF)


def column_lanes(nk, nj):
    tall = nj + 2
    lanes = -(-2 * nk * tall // 128) * 128
    return tall, lanes


def decode_matrix(nk, nj, ni, nx):
    tall, lanes = column_lanes(nk, nj)
    rows = np.arange(nk * nx)[:, None]
    cols = np.arange(2 * lanes)[None, :]
    c, lane = cols // lanes, cols % lanes
    side, k = lane // (nk * tall), lane // tall % nk
    x = np.where(side == 0, c, nx - 2 + c)
    beside = (side < 2) & (rows // nx == k) & (rows % nx == x)
    return np.concatenate([spread_matrix(nk, ni, nx), beside.astype(BF)], axis=1)


def stack_levels(read, levels, nk, zeros, lhs, at, rows, dz):
    for k in range(nk):
        level = SK * k - 1 + dz
        block = read(level) if 0 <= level < levels else zeros
        lhs[at : at + rows, k * 128 : (k + 1) * 128] = block


def pack_kernel(nk, vol, pick, dep, out, lhs, acc):
    v = pl.program_id(0)
    _, levels, ny, nx = vol.shape
    for dz in range(DZ):
        stack_levels(lambda l: vol[0, l].astype(BF), levels, nk, jnp.zeros((ny, nx), BF), lhs, dz * ny, ny, dz)
    part = jnp.dot(lhs[...], pick[0], preferred_element_type=F32)

    @pl.when(v == 0)
    def _():
        acc[...] = part

    @pl.when(v > 0)
    def _():
        acc[...] += part

    @pl.when(v == pl.num_programs(0) - 1)
    def _():
        out[...] = acc[...].astype(BF)


def im2col_kernel(nk, ni, nj, shard, with_own, vol, rim, edge, spread, edge_hot, dep, dep2, *refs):
    if with_own:
        own, weight, out, sums, lhs, q, w_buf, w_sem = refs
    else:
        out, lhs, q = refs
    v = pl.program_id(0)
    if with_own:
        copies = weight_copies(False, (weight,), 0, 0, w_buf, w_sem)

        @pl.when(v == 0)
        def _():
            for c in copies:
                c.start()

    _, levels, ny, nx = vol.shape
    main = DZ * ny
    for dz in range(DZ):
        stack_levels(lambda l: vol[0, l].astype(BF), levels, nk, jnp.zeros((ny, nx), BF), lhs, dz * ny, ny, dz)
    none = jnp.zeros((8, nx), F32)
    for k in range(nk):
        blocks = []
        for dz in range(DZ + 1):
            level = SK * k - 1 + dz
            blocks.append(rim[0, level] if 0 <= level < levels and dz < DZ else none)
        lhs[main : main + 64, k * 128 : (k + 1) * 128] = jnp.concatenate(blocks, axis=0).astype(BF)
    for pair in range(DX // 2):
        got = jnp.dot(lhs[...], spread[:, pair * 256 : (pair + 1) * 256], preferred_element_type=F32)
        if pair in (0, DX // 2 - 1):
            which = 0 if pair == 0 else 1
            got += jnp.dot(edge[...], edge_hot[0, :, which * 256 : (which + 1) * 256], preferred_element_type=F32)
        for h in range(2):
            dx = 2 * pair + h
            mine = got[:, h * 128 : (h + 1) * 128]
            for dz in range(DZ):
                q[dz, pl.ds(2 * DX + dx, ny, stride=DX), :] = mine[dz * ny : (dz + 1) * ny]
                at = main + 8 * dz
                q[dz, pl.ds(dx, 2, stride=DX), :] = mine[at : at + 2]
                q[dz, pl.ds(DX * (ny + 2) + dx, 2, stride=DX), :] = mine[at + 2 : at + 4]
    rows, padded, piece = shard
    head = piece * (GROUP - 1)
    per = SY * DX
    for j in range(nj):
        columns = jnp.concatenate([q[dz, per * j : per * j + DY * DX, :] for dz in range(DZ)], axis=0)
        gap = jnp.zeros((padded - rows, 128), F32)
        columns = jnp.concatenate([columns[:head], gap, columns[head:]], axis=0)
        out[0, j] = columns.T.astype(BF)
    if with_own:

        @pl.when(v == 0)
        def _():
            for c in copies:
                c.wait()

        @pl.when(v == own[0])
        def _():
            windows = out[0].reshape(nj * nk * ni, padded)
            sums[...] = jnp.dot(windows, w_buf[...], preferred_element_type=F32)


def weight_copies(gathered, sources, step, me, slot, sems):
    padded = slot.shape[0]
    piece = padded // GROUP
    if not gathered:
        (source,) = sources
        rows = source.shape[1]
        head = piece * (GROUP - 1)
        return [
            pltpu.make_async_copy(source.at[step, pl.ds(0, head)], slot.at[pl.ds(0, head)], sems.at[0]),
            pltpu.make_async_copy(source.at[step, pl.ds(rows - piece, piece)], slot.at[pl.ds(head, piece)], sems.at[1]),
        ]
    core = lax.rem(me, 2)
    a, b = 2 + 2 * core, 4 - 2 * core
    distances = ((0, a), (b, 6), (1, 1 + b), (1 + a, 7))
    copies = []
    for n, (source, pair) in enumerate(zip(sources, distances)):
        for h, distance in enumerate(pair):
            place = pl.multiple_of(lax.bitwise_xor(me, jnp.int32(distance)) * piece, piece)
            copies.append(
                pltpu.make_async_copy(source.at[h, step], slot.at[pl.ds(place, piece)], sems.at[2 * n + h])
            )
    return copies


def embed_kernel(n, gathered, first, vid, me, a, *refs):
    n_w = 4 if gathered else 1
    sources, refs = refs[:n_w], refs[n_w:]
    if not first:
        prev, refs = refs[0], refs[1:]
    out, a_buf, w_buf, acc, before, a_sem, w_sem, p_sem = refs

    def copies(s):
        slot = s % 2
        return [pltpu.make_async_copy(a.at[vid[s]], a_buf.at[slot], a_sem.at[slot])] + weight_copies(
            gathered, sources, s, me[0], w_buf.at[slot], w_sem.at[slot]
        )

    for c in copies(0):
        c.start()
    for s in range(n):
        for c in copies(s):
            c.wait()
        if s + 1 < n:
            for c in copies(s + 1):
                c.start()
        if s == max(n - 2, 0) and not first:
            extra = pltpu.make_async_copy(prev, before, p_sem)
            extra.start()
        got = jnp.dot(a_buf[s % 2], w_buf[s % 2], preferred_element_type=F32)
        if s > 0:
            got += acc[...]
        if s < n - 1:
            acc[...] = got
            continue
        if not first:
            extra.wait()
            got += before[...]
        nk, nj, ni, width = out.shape
        for j in range(nj):
            out[:, j] = got[j * nk * ni : (j + 1) * nk * ni].astype(BF).reshape(nk, ni, width)


def unembed_kernel(kinds, vid, me, tokens, above, below, left, right, hot_hbm, own, dep, *refs):
    gathered = any(kind is not None for kind in kinds)
    sources, refs = (refs[:4], refs[4:]) if gathered else ((), refs)
    if kinds[0] is not None:
        refs = refs[1:]
    vol, w_buf, t, t_side, r, q, qc, lhs, hot, w_sem, t_sem, hot_sem = refs
    s, n = pl.program_id(0), pl.num_programs(0)
    nk, nj, ni, width = tokens.shape
    _, levels, ny, nx = vol.shape
    per, over, block = SY * DX, (DY - SY) * DX, DY * DX
    padded = w_buf.shape[1]
    head, gap = padded // GROUP * (GROUP - 1), padded - DZ * block
    tall, c_lanes = column_lanes(nk, nj)
    half = nk * tall
    row = nk * ni
    c_at = (nj + 2) * row

    def copies(step, kind):
        slot = lax.rem(step, 2)
        if kind is None:
            return weight_copies(False, (own,), step, 0, w_buf.at[slot], w_sem.at[slot])
        return weight_copies(True, sources, kind + step, me[0], w_buf.at[slot], w_sem.at[slot])

    begin = None if kinds[0] is None else kinds[0]
    rest = None if kinds[-1] is None else kinds[-1] - len(kinds) + 1
    hot_copy = pltpu.make_async_copy(hot_hbm, hot, hot_sem)
    token_copies = [pltpu.make_async_copy(tokens.at[:, j], t.at[j], t_sem.at[j]) for j in range(nj)] + [
        pltpu.make_async_copy(above, t.at[nj], t_sem.at[nj]),
        pltpu.make_async_copy(below, t.at[nj + 1], t_sem.at[nj + 1]),
        pltpu.make_async_copy(left, t_side.at[pl.ds(0, half)], t_sem.at[nj + 2]),
        pltpu.make_async_copy(right, t_side.at[pl.ds(half, half)], t_sem.at[nj + 3]),
    ]

    @pl.when(s == 0)
    def _():
        for c in copies(s, begin) + token_copies:
            c.start()
        hot_copy.start()
        if c_lanes > 2 * half:
            t_side[2 * half :, :] = jnp.zeros((c_lanes - 2 * half, width), BF)

    @pl.when(s == 0)
    def _():
        for c in copies(s, begin) + token_copies:
            c.wait()

    @pl.when(s > 0)
    def _():
        for c in copies(s, rest):
            c.wait()

    @pl.when(s + 1 < n)
    def _():
        for c in copies(s + 1, rest):
            c.start()

    weight = w_buf[lax.rem(s, 2)]
    for ref, start, stop in ((t, 0, c_at), (t_side, c_at, c_at + c_lanes)):
        r[:, start:stop] = lax.dot_general(
            weight, ref[...].reshape(-1, width), (((1,), (1,)), ((), ())), preferred_element_type=F32
        )

    def rows_of(dz, at, start, stop, lanes=128):
        lo, hi = dz * block + start, dz * block + stop
        if hi <= head:
            return r[lo:hi, at : at + lanes]
        if lo >= head:
            return r[lo + gap : hi + gap, at : at + lanes]
        return jnp.concatenate([r[lo:head, at : at + lanes], r[head + gap : hi + gap, at : at + lanes]], axis=0)

    up, down = nj * row, (nj + 1) * row
    lane = lax.broadcasted_iota(jnp.int32, (8, c_lanes), 1)[:1]
    side, place = lane // half, lax.rem(lane, tall)
    edge2 = 2 * DX
    for dz in range(DZ):
        for j in range(nj + 1):
            at = per * j
            first, last = (edge2 if j == 0 else 0), (edge2 if j == nj else over)
            before = up if j == 0 else (j - 1) * row
            after = down if j == nj else j * row
            q[dz, at + first : at + last, :] = rows_of(dz, after, first, last) + rows_of(
                dz, before, per + first, per + last
            )
            qc[dz, at + first : at + last, :] = jnp.where(
                place == j + 1,
                rows_of(dz, c_at, first, last, c_lanes),
                jnp.where(place == j, rows_of(dz, c_at, per + first, per + last, c_lanes), 0.0),
            )
            if j < nj:
                q[dz, at + over : at + per, :] = rows_of(dz, after, over, per)
                qc[dz, at + over : at + per, :] = jnp.where(place == j + 1, rows_of(dz, c_at, over, per, c_lanes), 0.0)
    for dz in range(DZ):
        rows = slice(dz * ny, (dz + 1) * ny)
        for dx in range(DX):
            lhs[rows, dx * row : (dx + 1) * row] = q[dz, pl.ds(2 * DX + dx, ny, stride=DX), :].astype(BF)
        for c in range(2):
            far = qc[dz, pl.ds(2 * DX + DX - 2 + c, ny, stride=DX), :]
            near = qc[dz, pl.ds(2 * DX + c, ny, stride=DX), :]
            at = DX * row + c * c_lanes
            lhs[rows, at : at + c_lanes] = jnp.where(side == 0, far, near).astype(BF)

    @pl.when(s == 0)
    def _():
        hot_copy.wait()

    carry = None
    for pair in range(nk // 2):
        got = lax.dot_general(
            lhs[...], hot[pair * 256 : (pair + 1) * 256, :], (((1,), (1,)), ((), ())), preferred_element_type=F32
        )
        for h in range(2):
            k = 2 * pair + h
            mine = got[:, h * 128 : (h + 1) * 128]
            for dz in range(DZ):
                level = SK * k - 1 + dz
                here = mine[dz * ny : (dz + 1) * ny]
                if dz < DZ - SK and k > 0:
                    here = here + carry[dz]
                if 0 <= level < levels and (dz < SK or k == nk - 1):
                    vol[0, level] = here
            carry = [mine[dz * ny : (dz + 1) * ny] for dz in range(SK, DZ)]


def whole(shape):
    return pl.BlockSpec(shape, lambda *_: (0,) * len(shape))


def lead(shape):
    return pl.BlockSpec((1,) + tuple(shape[1:]), lambda v, *_: (v,) + (0,) * (len(shape) - 1))


HBM = pl.BlockSpec(memory_space=pltpu.HBM)


def cost(flops, bytes_accessed):
    return pl.CostEstimate(flops=int(flops), bytes_accessed=int(bytes_accessed), transcendentals=0)


def pack_edges(volume, nk, dep):
    nv, levels, ny, nx = volume.shape
    pick = pick_matrix(nv, nk, nx)
    return pl.pallas_call(
        functools.partial(pack_kernel, nk),
        grid=(nv,),
        in_specs=[lead(volume.shape), lead(pick.shape), HBM],
        out_specs=whole((DZ * ny, 128)),
        out_shape=jax.ShapeDtypeStruct((DZ * ny, 128), BF),
        scratch_shapes=[pltpu.VMEM((DZ * ny, nk * nx), BF), pltpu.VMEM((DZ * ny, 128), F32)],
        compiler_params=params(),
        cost_estimate=cost(2 * nv * DZ * ny * nk * nx * 256, volume.size * 4),
        name="pack_edges",
    )(volume, pick, dep)


def im2col(volume, rim, edge, spread, dims, own, weight, dep):
    nk, nj, ni, padded = dims
    nv, levels, ny, nx = volume.shape
    hot = edge_matrix(nv, nk, ni)
    rows = DZ * ny + 64
    shape = (nv, nj, nk * ni, padded)
    width = None if weight is None else weight.shape[-1]
    with_own = weight is not None
    extra_specs, extra, extra_out, extra_scratch = [], [], [], []
    if with_own:
        extra_specs, extra = [pl.BlockSpec(memory_space=pltpu.SMEM), HBM], [own, weight]
        extra_out = [(nj * nk * ni, width)]
        extra_scratch = [pltpu.VMEM((padded, width), BF), pltpu.SemaphoreType.DMA((2,))]
    return pl.pallas_call(
        functools.partial(im2col_kernel, nk, ni, nj, (DZ * DY * DX, padded, padded // GROUP), with_own),
        grid=(nv,),
        in_specs=[lead(volume.shape), lead(rim.shape), whole(edge.shape), whole(spread.shape), lead(hot.shape), HBM, HBM]
        + extra_specs,
        out_specs=[lead(shape)] + [whole(x) for x in extra_out],
        out_shape=[jax.ShapeDtypeStruct(shape, BF)] + [jax.ShapeDtypeStruct(x, F32) for x in extra_out],
        scratch_shapes=[pltpu.VMEM((rows, nk * nx), BF), pltpu.VMEM((DZ, DX * (ny + 4), 128), F32)] + extra_scratch,
        compiler_params=params(),
        cost_estimate=cost(3 * nv * rows * nk * nx * DX * 128, volume.size * 4 + 2 * nv * nj * 128 * padded),
        name="im2col",
    )(volume, rim, edge, spread, hot, *dep, *extra)


def embed(a, weights, vid, me, prev, gathered, token_shape):
    n = vid.shape[0]
    nv, rows, padded = a.shape
    width = weights[0].shape[-1]
    first = prev is None
    smem = pl.BlockSpec(memory_space=pltpu.SMEM)
    return pl.pallas_call(
        functools.partial(embed_kernel, n, gathered, first),
        in_specs=[smem, smem, HBM] + [HBM] * (len(weights) + (not first)),
        out_specs=pl.BlockSpec(memory_space=pltpu.VMEM),
        out_shape=jax.ShapeDtypeStruct(token_shape, BF),
        scratch_shapes=[
            pltpu.VMEM((2, rows, padded), BF),
            pltpu.VMEM((2, padded, width), BF),
            pltpu.VMEM((rows, width), F32),
            pltpu.VMEM((8, 128) if first else (rows, width), F32),
            pltpu.SemaphoreType.DMA((2,)),
            pltpu.SemaphoreType.DMA((2, GROUP)),
            pltpu.SemaphoreType.DMA,
        ],
        compiler_params=params(),
        cost_estimate=cost(2 * n * rows * padded * width, 2 * n * padded * (rows + width) + 4 * rows * width),
        name="embed",
    )(vid, me, a, *weights, *([] if first else [prev]))


def unembed(tokens, beside, own, gathered, kinds, vid, me, prev, dep, volume_shape, padded):
    nk, nj, ni, width = tokens.shape
    nv, levels, ny, nx = volume_shape
    hot = decode_matrix(nk, nj, ni, nx)
    tall, c_lanes = column_lanes(nk, nj)
    before = () if prev is None else (prev,)
    n = len(kinds)
    count = (nj + 2) * nk * ni + c_lanes
    return pl.pallas_call(
        functools.partial(unembed_kernel, kinds),
        grid_spec=pltpu.PrefetchScalarGridSpec(
            num_scalar_prefetch=2,
            grid=(len(kinds),),
            in_specs=[HBM] * (4 + len(beside) + len(gathered) + len(before)),
            out_specs=pl.BlockSpec((1, levels, ny, nx), lambda s, vid, me: (vid[s], 0, 0, 0)),
            scratch_shapes=[
                pltpu.VMEM((2, padded, width), BF),
                pltpu.VMEM((nj + 2, nk, ni, width), BF),
                pltpu.VMEM((c_lanes, width), BF),
                pltpu.VMEM((padded, count), F32),
                pltpu.VMEM((DZ, DX * (ny + 4), nk * ni), F32),
                pltpu.VMEM((DZ, DX * (ny + 4), c_lanes), F32),
                pltpu.VMEM((DZ * ny, hot.shape[1]), BF),
                pltpu.VMEM(hot.shape, BF),
                pltpu.SemaphoreType.DMA((2, GROUP)),
                pltpu.SemaphoreType.DMA((nj + 4,)),
                pltpu.SemaphoreType.DMA,
            ],
        ),
        out_shape=jax.ShapeDtypeStruct(volume_shape, F32),
        input_output_aliases={} if prev is None else {len(beside) + 6 + len(gathered): 0},
        compiler_params=params(),
        cost_estimate=cost(8 * n * padded * width * nj * 128, 2 * n * padded * width + 4 * n * levels * ny * nx),
        name="unembed",
    )(vid, me, tokens, *beside, hot, own, dep, *gathered, *before)


def both_ways(up_rows, down_rows, axis, wrap):
    size = lax.axis_size(axis)
    up = [(i, (i + 1) % size) for i in range(size if wrap else size - 1)]
    return lax.ppermute(up_rows, axis, up), lax.ppermute(down_rows, axis, [(j, i) for i, j in up])


def piece_rows(rows):
    return -(-rows // (16 * GROUP)) * 16


def after(x, *others):
    return lax.optimization_barrier((x,) + others)[0]


def own_piece(weight, me):
    rows, piece = weight.shape[0], piece_rows(weight.shape[0])
    return lax.dynamic_slice_in_dim(weight, jnp.minimum(me * piece, rows - piece), piece, 0)


def from_lat(piece):
    size = lax.axis_size("lat")
    got = [lax.ppermute(piece, "lat", [(i, (i + s) % size) for i in range(size)]) for s in range(1, size)]
    return got


def flip(x, mask):
    return lax.ppermute(x, "lon", [(i, i ^ mask(i)) for i in range(lax.axis_size("lon"))])


def first_mask(i):
    return 2 + 2 * (i & 1)


def second_mask(i):
    return 4 - 2 * (i & 1)


def core_mask(i):
    return 1


def per_device(volume_b, tokens_a, embed_weight, unembed_weight):
    nk, nj, ni, width = tokens_a.shape
    nv, levels, ny, nx = volume_b.shape
    rows = DZ * DY * DX
    padded = piece_rows(rows) * GROUP
    main = DZ * ny
    lat, lats = lax.axis_index("lat"), lax.axis_size("lat")
    me = lax.rem(lax.axis_index("lon"), GROUP).astype(jnp.int32)
    me1 = me.reshape(1)
    fast = embed_weight.shape[0] == rows and lax.axis_size("lon") % GROUP == 0
    spread = spread_matrix(nk, ni, nx)

    row_above, row_below = both_ways(tokens_a[:, nj - 1], tokens_a[:, 0], "lat", False)

    start = volume_b
    if fast:
        start = own_piece(unembed_weight, me)
        u_near = from_lat(start)
    packed = pack_edges(volume_b, nk, start)
    from_left, from_right = both_ways(packed, packed, "lon", True)

    def column(i):
        return jnp.concatenate([row_above[:, i][:, None], tokens_a[:, :, i], row_below[:, i][:, None]], axis=1)

    left, right = both_ways(column(ni - 1), column(0), "lon", True)
    beside = [row_above, row_below, left.reshape(-1, width), right.reshape(-1, width)]

    def lat_rows(at):
        voxels = volume_b[:, :, at : at + 2].astype(BF).reshape(-1, nx)
        corners = [a.reshape(DZ, ny, 128)[:, at : at + 2].reshape(-1, 128) for a in (from_left, from_right)]
        return jnp.concatenate([voxels] + corners, axis=0)

    above, below = both_ways(lat_rows(ny - 2), lat_rows(0), "lat", False)
    n_vox = nv * levels * 2

    def split(got):
        voxels = got[:n_vox].reshape(nv, levels, 2, nx)
        corners = got[n_vox:].reshape(2, DZ, 2, 128)
        return voxels, jnp.concatenate([corners[0], corners[1]], axis=-1)

    (vox_above, cor_above), (vox_below, cor_below) = split(above), split(below)
    rim = jnp.concatenate([vox_above, vox_below, jnp.zeros((nv, levels, 4, nx), BF)], axis=2).astype(F32)
    corners = jnp.concatenate([cor_above, cor_below, jnp.zeros((DZ, 4, 256), BF)], axis=1).reshape(8 * DZ, 256)
    edge = jnp.concatenate(
        [jnp.concatenate([from_left, from_right], axis=1), corners, jnp.zeros((64 - 8 * DZ, 256), BF)], axis=0
    )
    dims = (nk, nj, ni, padded)
    tokens = nj * nk * ni

    if fast:
        u_near = jnp.stack(u_near)
        u_pair = jnp.stack([u_near, after(flip(u_near, first_mask), row_above, row_below)])
        u_rest = flip(u_pair, second_mask)
        e_near = from_lat(after(own_piece(embed_weight, me), u_near))
        own = lat.astype(jnp.int32).reshape(1)
        others = lax.rem(lat - jnp.arange(1, lats, dtype=jnp.int32) + lats, lats).astype(jnp.int32)
        a, sums = im2col(volume_b, rim, edge, spread, dims, own, embed_weight[None], (u_pair, edge))
        u_rest = after(u_rest, sums)
        u_all = (u_pair, u_rest, flip(u_pair, core_mask), flip(u_rest, core_mask))
        e_near = jnp.stack(e_near)
        e_far = flip(after(e_near, sums), first_mask)
        first_two = jnp.concatenate([own, others[:1]])
        volume_a = unembed(
            tokens_a, beside, unembed_weight[None], u_all, (None, 0), first_two, me1, None, e_near, volume_b.shape, padded
        )
        e_pair = jnp.stack([e_near, after(e_far, volume_a)])
        e_rest = flip(e_pair, second_mask)
        volume_a = unembed(
            tokens_a, beside, unembed_weight[None], u_all, (1, 2), others[1:], me1, volume_a, e_pair, volume_b.shape, padded
        )
        e_rest = after(e_rest, volume_a)
        e_all = (e_pair, e_rest, flip(e_pair, core_mask), flip(e_rest, core_mask))
        tokens_b = embed(a.reshape(nv, tokens, padded), e_all, others, me1, sums, True, tokens_a.shape)
    else:
        every = jnp.arange(nv, dtype=jnp.int32)
        decode, encode = (
            lax.all_gather(w, "lat", axis=0, tiled=True).reshape(nv, rows, width)
            for w in (unembed_weight, embed_weight)
        )
        (a,) = im2col(volume_b, rim, edge, spread, dims, None, None, (edge, edge))
        volume_a = unembed(
            tokens_a, beside, decode, (), (None,) * nv, every, me1, None, edge, volume_b.shape, padded
        )
        tokens_b = embed(
            a.reshape(nv, tokens, padded), (encode,), every, me1, None, False, tokens_a.shape
        )
    return tokens_b, volume_a


def solution(mesh):
    placed = (
        P(None, None, "lat", "lon"),
        P(None, "lat", "lon", None),
        P("lat", None),
        P("lat", None),
    )
    return jax.shard_map(
        per_device,
        mesh=mesh,
        in_specs=placed,
        out_specs=(P(None, "lat", "lon", None), P(None, None, "lat", "lon")),
        check_vma=False,
    )
```

```python
import functools

import jax
import jax.numpy as jnp
import numpy as np
from jax import lax
from jax.experimental import pallas as pl
from jax.experimental.pallas import tpu as pltpu
from jax.sharding import PartitionSpec as P

BF = jnp.bfloat16
F32 = jnp.float32
VMEM_LIMIT = 56 * 1024 * 1024
DZ, DY, DX = 7, 12, 12
SK, SY, SX = 5, 8, 8
GROUP = 8


def params():
    return pltpu.CompilerParams(vmem_limit_bytes=VMEM_LIMIT)


def spread_matrix(nk, ni, nx):
    rows = np.arange(nk * nx)[:, None]
    cols = np.arange(DX * nk * ni)[None, :]
    dx, k, i = cols // (nk * ni), cols // ni % nk, cols % ni
    return ((rows // nx == k) & (rows % nx == SX * i - 2 + dx)).astype(BF)


def edge_lanes(nv, nk):
    lane = np.arange(4 * nv * nk)
    return lane // (2 * nv * nk), lane // (2 * nk) % nv, lane // nk % 2, lane % nk


def pick_matrix(nv, nk, nx):
    side, v, c, k = edge_lanes(nv, nk)
    rows = np.arange(nk * nx)[None, :, None]
    x = np.where(side == 0, nx - 2 + c, c)
    own = np.arange(nv)[:, None, None] == v
    return (own & (rows // nx == k) & (rows % nx == x)).astype(BF)


def edge_matrix(nv, nk, ni):
    side, v, c, k = (np.tile(a, 2)[None, :, None] for a in edge_lanes(nv, nk))
    half = (np.arange(8 * nv * nk) // (4 * nv * nk))[None, :, None]
    cols = np.arange(4 * nk * ni)[None, None, :]
    d, kk, i = cols // (nk * ni), cols // ni % nk, cols % ni
    own = np.arange(nv)[:, None, None] == v
    left = (half == 0) & (side == 0) & (i == 0) & (d == c)
    right = (half == 1) & (side == 1) & (i == ni - 1) & (d == 2 + c)
    return (own & (k == kk) & (left | right)).astype(BF)


def column_lanes(nk, nj):
    tall = nj + 2
    lanes = -(-2 * nk * tall // 128) * 128
    return tall, lanes


def decode_matrix(nk, nj, ni, nx):
    tall, lanes = column_lanes(nk, nj)
    rows = np.arange(nk * nx)[:, None]
    cols = np.arange(2 * lanes)[None, :]
    c, lane = cols // lanes, cols % lanes
    side, k = lane // (nk * tall), lane // tall % nk
    x = np.where(side == 0, c, nx - 2 + c)
    beside = (side < 2) & (rows // nx == k) & (rows % nx == x)
    return np.concatenate([spread_matrix(nk, ni, nx), beside.astype(BF)], axis=1)


def stack_levels(read, levels, nk, zeros, lhs, at, rows, dz):
    for k in range(nk):
        level = SK * k - 1 + dz
        block = read(level) if 0 <= level < levels else zeros
        lhs[at : at + rows, k * 128 : (k + 1) * 128] = block


def stack_rim(rim, levels, nk, lhs, main):
    none = jnp.zeros((8, rim.shape[3]), F32)
    for k in range(nk):
        blocks = []
        for dz in range(DZ + 1):
            level = SK * k - 1 + dz
            blocks.append(rim[0, level] if 0 <= level < levels and dz < DZ else none)
        lhs[main : main + 64, k * 128 : (k + 1) * 128] = jnp.concatenate(blocks, axis=0).astype(BF)


def pack_kernel(nk, vol, rim, pick, dep, out, lhs, acc):
    v = pl.program_id(0)
    _, levels, ny, nx = vol.shape
    for dz in range(DZ):
        stack_levels(lambda l: vol[0, l].astype(BF), levels, nk, jnp.zeros((ny, nx), BF), lhs, dz * ny, ny, dz)
    stack_rim(rim, levels, nk, lhs, DZ * ny)
    part = jnp.dot(lhs[...], pick[0], preferred_element_type=F32)

    @pl.when(v == 0)
    def _():
        acc[...] = part

    @pl.when(v > 0)
    def _():
        acc[...] += part

    @pl.when(v == pl.num_programs(0) - 1)
    def _():
        out[...] = acc[...].astype(BF)


def im2col_kernel(nk, ni, nj, shard, with_own, vol, rim, edge, spread, edge_hot, dep, dep2, *refs):
    if with_own:
        own, weight, out, sums, lhs, q, w_buf, w_sem = refs
    else:
        out, lhs, q = refs
    v = pl.program_id(0)
    if with_own:
        copies = weight_copies(False, (weight,), 0, 0, w_buf, w_sem)

        @pl.when(v == 0)
        def _():
            for c in copies:
                c.start()

    _, levels, ny, nx = vol.shape
    main = DZ * ny
    for dz in range(DZ):
        stack_levels(lambda l: vol[0, l].astype(BF), levels, nk, jnp.zeros((ny, nx), BF), lhs, dz * ny, ny, dz)
    stack_rim(rim, levels, nk, lhs, main)
    for pair in range(DX // 2):
        got = jnp.dot(lhs[...], spread[:, pair * 256 : (pair + 1) * 256], preferred_element_type=F32)
        if pair in (0, DX // 2 - 1):
            which = 0 if pair == 0 else 1
            got += jnp.dot(edge[...], edge_hot[0, :, which * 256 : (which + 1) * 256], preferred_element_type=F32)
        for h in range(2):
            dx = 2 * pair + h
            mine = got[:, h * 128 : (h + 1) * 128]
            for dz in range(DZ):
                q[dz, pl.ds(2 * DX + dx, ny, stride=DX), :] = mine[dz * ny : (dz + 1) * ny]
                at = main + 8 * dz
                q[dz, pl.ds(dx, 2, stride=DX), :] = mine[at : at + 2]
                q[dz, pl.ds(DX * (ny + 2) + dx, 2, stride=DX), :] = mine[at + 2 : at + 4]
    rows, padded, piece = shard
    head = piece * (GROUP - 1)
    per = SY * DX
    for j in range(nj):
        columns = jnp.concatenate([q[dz, per * j : per * j + DY * DX, :] for dz in range(DZ)], axis=0)
        gap = jnp.zeros((padded - rows, 128), F32)
        columns = jnp.concatenate([columns[:head], gap, columns[head:]], axis=0)
        out[0, j] = columns.T.astype(BF)
    if with_own:

        @pl.when(v == 0)
        def _():
            for c in copies:
                c.wait()

        @pl.when(v == own[0])
        def _():
            windows = out[0].reshape(nj * nk * ni, padded)
            sums[...] = jnp.dot(windows, w_buf[...], preferred_element_type=F32)


def weight_copies(gathered, sources, step, me, slot, sems):
    padded = slot.shape[0]
    piece = padded // GROUP
    if not gathered:
        (source,) = sources
        rows = source.shape[1]
        head = piece * (GROUP - 1)
        return [
            pltpu.make_async_copy(source.at[step, pl.ds(0, head)], slot.at[pl.ds(0, head)], sems.at[0]),
            pltpu.make_async_copy(source.at[step, pl.ds(rows - piece, piece)], slot.at[pl.ds(head, piece)], sems.at[1]),
        ]
    core = lax.rem(me, 2)
    a, b = 2 + 2 * core, 4 - 2 * core
    distances = ((0, a), (b, 6), (1, 1 + b), (1 + a, 7))
    copies = []
    for n, (source, pair) in enumerate(zip(sources, distances)):
        for h, distance in enumerate(pair):
            place = pl.multiple_of(lax.bitwise_xor(me, jnp.int32(distance)) * piece, piece)
            copies.append(
                pltpu.make_async_copy(source.at[h, step], slot.at[pl.ds(place, piece)], sems.at[2 * n + h])
            )
    return copies


def embed_kernel(n, gathered, first, vid, me, a, *refs):
    n_w = 4 if gathered else 1
    sources, refs = refs[:n_w], refs[n_w:]
    if not first:
        prev, refs = refs[0], refs[1:]
    out, a_buf, w_buf, acc, before, a_sem, w_sem, p_sem = refs

    def copies(s):
        slot = s % 2
        return [pltpu.make_async_copy(a.at[vid[s]], a_buf.at[slot], a_sem.at[slot])] + weight_copies(
            gathered, sources, s, me[0], w_buf.at[slot], w_sem.at[slot]
        )

    for c in copies(0):
        c.start()
    for s in range(n):
        for c in copies(s):
            c.wait()
        if s + 1 < n:
            for c in copies(s + 1):
                c.start()
        if s == max(n - 2, 0) and not first:
            extra = pltpu.make_async_copy(prev, before, p_sem)
            extra.start()
        got = jnp.dot(a_buf[s % 2], w_buf[s % 2], preferred_element_type=F32)
        if s > 0:
            got += acc[...]
        if s < n - 1:
            acc[...] = got
            continue
        if not first:
            extra.wait()
            got += before[...]
        nk, nj, ni, width = out.shape
        for j in range(nj):
            out[:, j] = got[j * nk * ni : (j + 1) * nk * ni].astype(BF).reshape(nk, ni, width)


def unembed_kernel(kinds, vid, me, tokens, above, below, left, right, hot_hbm, own, dep, *refs):
    gathered = any(kind is not None for kind in kinds)
    sources, refs = (refs[:4], refs[4:]) if gathered else ((), refs)
    if kinds[0] is not None:
        refs = refs[1:]
    vol, w_buf, t, t_side, r, q, qc, lhs, hot, w_sem, t_sem, hot_sem = refs
    s, n = pl.program_id(0), pl.num_programs(0)
    nk, nj, ni, width = tokens.shape
    _, levels, ny, nx = vol.shape
    per, over, block = SY * DX, (DY - SY) * DX, DY * DX
    padded = w_buf.shape[1]
    head, gap = padded // GROUP * (GROUP - 1), padded - DZ * block
    tall, c_lanes = column_lanes(nk, nj)
    half = nk * tall
    row = nk * ni
    c_at = (nj + 2) * row

    def copies(step, kind):
        slot = lax.rem(step, 2)
        if kind is None:
            return weight_copies(False, (own,), step, 0, w_buf.at[slot], w_sem.at[slot])
        return weight_copies(True, sources, kind + step, me[0], w_buf.at[slot], w_sem.at[slot])

    begin = None if kinds[0] is None else kinds[0]
    rest = None if kinds[-1] is None else kinds[-1] - len(kinds) + 1
    hot_copy = pltpu.make_async_copy(hot_hbm, hot, hot_sem)
    token_copies = [pltpu.make_async_copy(tokens.at[:, j], t.at[j], t_sem.at[j]) for j in range(nj)] + [
        pltpu.make_async_copy(above, t.at[nj], t_sem.at[nj]),
        pltpu.make_async_copy(below, t.at[nj + 1], t_sem.at[nj + 1]),
        pltpu.make_async_copy(left, t_side.at[pl.ds(0, half)], t_sem.at[nj + 2]),
        pltpu.make_async_copy(right, t_side.at[pl.ds(half, half)], t_sem.at[nj + 3]),
    ]

    @pl.when(s == 0)
    def _():
        for c in copies(s, begin) + token_copies:
            c.start()
        hot_copy.start()
        if c_lanes > 2 * half:
            t_side[2 * half :, :] = jnp.zeros((c_lanes - 2 * half, width), BF)

    @pl.when(s == 0)
    def _():
        for c in copies(s, begin) + token_copies:
            c.wait()

    @pl.when(s > 0)
    def _():
        for c in copies(s, rest):
            c.wait()

    @pl.when(s + 1 < n)
    def _():
        for c in copies(s + 1, rest):
            c.start()

    weight = w_buf[lax.rem(s, 2)]
    for ref, start, stop in ((t, 0, c_at), (t_side, c_at, c_at + c_lanes)):
        r[:, start:stop] = lax.dot_general(
            weight, ref[...].reshape(-1, width), (((1,), (1,)), ((), ())), preferred_element_type=F32
        )

    def rows_of(dz, at, start, stop, lanes=128):
        lo, hi = dz * block + start, dz * block + stop
        if hi <= head:
            return r[lo:hi, at : at + lanes]
        if lo >= head:
            return r[lo + gap : hi + gap, at : at + lanes]
        return jnp.concatenate([r[lo:head, at : at + lanes], r[head + gap : hi + gap, at : at + lanes]], axis=0)

    up, down = nj * row, (nj + 1) * row
    lane = lax.broadcasted_iota(jnp.int32, (8, c_lanes), 1)[:1]
    side, place = lane // half, lax.rem(lane, tall)
    edge2 = 2 * DX
    for dz in range(DZ):
        for j in range(nj + 1):
            at = per * j
            first, last = (edge2 if j == 0 else 0), (edge2 if j == nj else over)
            before = up if j == 0 else (j - 1) * row
            after = down if j == nj else j * row
            q[dz, at + first : at + last, :] = rows_of(dz, after, first, last) + rows_of(
                dz, before, per + first, per + last
            )
            qc[dz, at + first : at + last, :] = jnp.where(
                place == j + 1,
                rows_of(dz, c_at, first, last, c_lanes),
                jnp.where(place == j, rows_of(dz, c_at, per + first, per + last, c_lanes), 0.0),
            )
            if j < nj:
                q[dz, at + over : at + per, :] = rows_of(dz, after, over, per)
                qc[dz, at + over : at + per, :] = jnp.where(place == j + 1, rows_of(dz, c_at, over, per, c_lanes), 0.0)
    for dz in range(DZ):
        rows = slice(dz * ny, (dz + 1) * ny)
        for dx in range(DX):
            lhs[rows, dx * row : (dx + 1) * row] = q[dz, pl.ds(2 * DX + dx, ny, stride=DX), :].astype(BF)
        for c in range(2):
            far = qc[dz, pl.ds(2 * DX + DX - 2 + c, ny, stride=DX), :]
            near = qc[dz, pl.ds(2 * DX + c, ny, stride=DX), :]
            at = DX * row + c * c_lanes
            lhs[rows, at : at + c_lanes] = jnp.where(side == 0, far, near).astype(BF)

    @pl.when(s == 0)
    def _():
        hot_copy.wait()

    carry = None
    for pair in range(nk // 2):
        got = lax.dot_general(
            lhs[...], hot[pair * 256 : (pair + 1) * 256, :], (((1,), (1,)), ((), ())), preferred_element_type=F32
        )
        for h in range(2):
            k = 2 * pair + h
            mine = got[:, h * 128 : (h + 1) * 128]
            for dz in range(DZ):
                level = SK * k - 1 + dz
                here = mine[dz * ny : (dz + 1) * ny]
                if dz < DZ - SK and k > 0:
                    here = here + carry[dz]
                if 0 <= level < levels and (dz < SK or k == nk - 1):
                    vol[0, level] = here
            carry = [mine[dz * ny : (dz + 1) * ny] for dz in range(SK, DZ)]


def whole(shape):
    return pl.BlockSpec(shape, lambda *_: (0,) * len(shape))


def lead(shape):
    return pl.BlockSpec((1,) + tuple(shape[1:]), lambda v, *_: (v,) + (0,) * (len(shape) - 1))


HBM = pl.BlockSpec(memory_space=pltpu.HBM)


def cost(flops, bytes_accessed):
    return pl.CostEstimate(flops=int(flops), bytes_accessed=int(bytes_accessed), transcendentals=0)


def pack_edges(volume, rim, nk, dep):
    nv, levels, ny, nx = volume.shape
    pick = pick_matrix(nv, nk, nx)
    rows = DZ * ny + 64
    return pl.pallas_call(
        functools.partial(pack_kernel, nk),
        grid=(nv,),
        in_specs=[lead(volume.shape), lead(rim.shape), lead(pick.shape), HBM],
        out_specs=whole((rows, 128)),
        out_shape=jax.ShapeDtypeStruct((rows, 128), BF),
        scratch_shapes=[pltpu.VMEM((rows, nk * nx), BF), pltpu.VMEM((rows, 128), F32)],
        compiler_params=params(),
        cost_estimate=cost(2 * nv * DZ * ny * nk * nx * 256, volume.size * 4),
        name="pack_edges",
    )(volume, rim, pick, dep)


def im2col(volume, rim, edge, spread, dims, own, weight, dep):
    nk, nj, ni, padded = dims
    nv, levels, ny, nx = volume.shape
    hot = edge_matrix(nv, nk, ni)
    rows = DZ * ny + 64
    shape = (nv, nj, nk * ni, padded)
    width = None if weight is None else weight.shape[-1]
    with_own = weight is not None
    extra_specs, extra, extra_out, extra_scratch = [], [], [], []
    if with_own:
        extra_specs, extra = [pl.BlockSpec(memory_space=pltpu.SMEM), HBM], [own, weight]
        extra_out = [(nj * nk * ni, width)]
        extra_scratch = [pltpu.VMEM((padded, width), BF), pltpu.SemaphoreType.DMA((2,))]
    return pl.pallas_call(
        functools.partial(im2col_kernel, nk, ni, nj, (DZ * DY * DX, padded, padded // GROUP), with_own),
        grid=(nv,),
        in_specs=[lead(volume.shape), lead(rim.shape), whole(edge.shape), whole(spread.shape), lead(hot.shape), HBM, HBM]
        + extra_specs,
        out_specs=[lead(shape)] + [whole(x) for x in extra_out],
        out_shape=[jax.ShapeDtypeStruct(shape, BF)] + [jax.ShapeDtypeStruct(x, F32) for x in extra_out],
        scratch_shapes=[pltpu.VMEM((rows, nk * nx), BF), pltpu.VMEM((DZ, DX * (ny + 4), 128), F32)] + extra_scratch,
        compiler_params=params(),
        cost_estimate=cost(3 * nv * rows * nk * nx * DX * 128, volume.size * 4 + 2 * nv * nj * 128 * padded),
        name="im2col",
    )(volume, rim, edge, spread, hot, *dep, *extra)


def embed(a, weights, vid, me, prev, gathered, token_shape):
    n = vid.shape[0]
    nv, rows, padded = a.shape
    width = weights[0].shape[-1]
    first = prev is None
    smem = pl.BlockSpec(memory_space=pltpu.SMEM)
    return pl.pallas_call(
        functools.partial(embed_kernel, n, gathered, first),
        in_specs=[smem, smem, HBM] + [HBM] * (len(weights) + (not first)),
        out_specs=pl.BlockSpec(memory_space=pltpu.VMEM),
        out_shape=jax.ShapeDtypeStruct(token_shape, BF),
        scratch_shapes=[
            pltpu.VMEM((2, rows, padded), BF),
            pltpu.VMEM((2, padded, width), BF),
            pltpu.VMEM((rows, width), F32),
            pltpu.VMEM((8, 128) if first else (rows, width), F32),
            pltpu.SemaphoreType.DMA((2,)),
            pltpu.SemaphoreType.DMA((2, GROUP)),
            pltpu.SemaphoreType.DMA,
        ],
        compiler_params=params(),
        cost_estimate=cost(2 * n * rows * padded * width, 2 * n * padded * (rows + width) + 4 * rows * width),
        name="embed",
    )(vid, me, a, *weights, *([] if first else [prev]))


def unembed(tokens, beside, own, gathered, kinds, vid, me, prev, dep, volume_shape, padded):
    nk, nj, ni, width = tokens.shape
    nv, levels, ny, nx = volume_shape
    hot = decode_matrix(nk, nj, ni, nx)
    tall, c_lanes = column_lanes(nk, nj)
    before = () if prev is None else (prev,)
    n = len(kinds)
    count = (nj + 2) * nk * ni + c_lanes
    return pl.pallas_call(
        functools.partial(unembed_kernel, kinds),
        grid_spec=pltpu.PrefetchScalarGridSpec(
            num_scalar_prefetch=2,
            grid=(len(kinds),),
            in_specs=[HBM] * (4 + len(beside) + len(gathered) + len(before)),
            out_specs=pl.BlockSpec((1, levels, ny, nx), lambda s, vid, me: (vid[s], 0, 0, 0)),
            scratch_shapes=[
                pltpu.VMEM((2, padded, width), BF),
                pltpu.VMEM((nj + 2, nk, ni, width), BF),
                pltpu.VMEM((c_lanes, width), BF),
                pltpu.VMEM((padded, count), F32),
                pltpu.VMEM((DZ, DX * (ny + 4), nk * ni), F32),
                pltpu.VMEM((DZ, DX * (ny + 4), c_lanes), F32),
                pltpu.VMEM((DZ * ny, hot.shape[1]), BF),
                pltpu.VMEM(hot.shape, BF),
                pltpu.SemaphoreType.DMA((2, GROUP)),
                pltpu.SemaphoreType.DMA((nj + 4,)),
                pltpu.SemaphoreType.DMA,
            ],
        ),
        out_shape=jax.ShapeDtypeStruct(volume_shape, F32),
        input_output_aliases={} if prev is None else {len(beside) + 6 + len(gathered): 0},
        compiler_params=params(),
        cost_estimate=cost(1000, 1000) if n == 1 else cost(8 * n * padded * width * nj * 128, 2 * n * padded * width + 4 * n * levels * ny * nx),
        name="unembed",
    )(vid, me, tokens, *beside, hot, own, dep, *gathered, *before)


def both_ways(up_rows, down_rows, axis, wrap):
    size = lax.axis_size(axis)
    up = [(i, (i + 1) % size) for i in range(size if wrap else size - 1)]
    return lax.ppermute(up_rows, axis, up), lax.ppermute(down_rows, axis, [(j, i) for i, j in up])


def piece_rows(rows):
    return -(-rows // (16 * GROUP)) * 16


def after(x, *others):
    return lax.optimization_barrier((x,) + others)[0]


def own_piece(weight, me):
    rows, piece = weight.shape[0], piece_rows(weight.shape[0])
    return lax.dynamic_slice_in_dim(weight, jnp.minimum(me * piece, rows - piece), piece, 0)


def from_lat(piece):
    size = lax.axis_size("lat")
    got = [lax.ppermute(piece, "lat", [(i, (i + s) % size) for i in range(size)]) for s in range(1, size)]
    return got


def flip(x, mask):
    return lax.ppermute(x, "lon", [(i, i ^ mask(i)) for i in range(lax.axis_size("lon"))])


def first_mask(i):
    return 2 + 2 * (i & 1)


def second_mask(i):
    return 4 - 2 * (i & 1)


def core_mask(i):
    return 1


def per_device(volume_b, tokens_a, embed_weight, unembed_weight):
    nk, nj, ni, width = tokens_a.shape
    nv, levels, ny, nx = volume_b.shape
    rows = DZ * DY * DX
    padded = piece_rows(rows) * GROUP
    main = DZ * ny
    lat, lats = lax.axis_index("lat"), lax.axis_size("lat")
    me = lax.rem(lax.axis_index("lon"), GROUP).astype(jnp.int32)
    me1 = me.reshape(1)
    fast = embed_weight.shape[0] == rows and lax.axis_size("lon") % GROUP == 0
    spread = spread_matrix(nk, ni, nx)

    def voxels(at):
        return volume_b[:, :, at : at + 2].astype(BF).reshape(-1, nx)

    above, below = (x.reshape(nv, levels, 2, nx) for x in both_ways(voxels(ny - 2), voxels(0), "lat", False))
    rim = jnp.concatenate([above, below, jnp.zeros((nv, levels, 4, nx), BF)], axis=2).astype(F32)
    row_above, row_below = both_ways(tokens_a[:, nj - 1], tokens_a[:, 0], "lat", False)

    start = volume_b
    if fast:
        start = own_piece(unembed_weight, me)
        u_near = from_lat(start)
    packed = pack_edges(volume_b, rim, nk, start)
    edge = jnp.concatenate(both_ways(packed, packed, "lon", True), axis=1)

    def column(i):
        return jnp.concatenate([row_above[:, i][:, None], tokens_a[:, :, i], row_below[:, i][:, None]], axis=1)

    left, right = both_ways(column(ni - 1), column(0), "lon", True)
    beside = [row_above, row_below, left.reshape(-1, width), right.reshape(-1, width)]
    dims = (nk, nj, ni, padded)
    tokens = nj * nk * ni

    if fast:
        u_near = jnp.stack(u_near)
        u_pair = jnp.stack([u_near, after(flip(u_near, first_mask), row_above, row_below)])
        u_rest = flip(u_pair, second_mask)
        e_got = from_lat(after(own_piece(embed_weight, me), u_near))
        own = lat.astype(jnp.int32).reshape(1)
        others = lax.rem(lat - jnp.arange(1, lats, dtype=jnp.int32) + lats, lats).astype(jnp.int32)
        a, sums = im2col(volume_b, rim, edge, spread, dims, own, embed_weight[None], (u_pair, edge))
        u_rest = after(u_rest, sums)
        u_all = (u_pair, u_rest, flip(u_pair, core_mask), flip(u_rest, core_mask))
        first_two = jnp.concatenate([own, others[:1]])
        volume_a = unembed(
            tokens_a, beside, unembed_weight[None], (), (None,), own, me1, None, sums, volume_b.shape, padded
        )
        e_near = jnp.stack([after(x, volume_a) for x in e_got])
        e_far = flip(e_near, first_mask)
        volume_a = unembed(
            tokens_a, beside, unembed_weight[None], u_all, (0,), others[:1], me1, volume_a, e_near, volume_b.shape, padded
        )
        e_pair = jnp.stack([e_near, after(e_far, volume_a)])
        e_rest = flip(e_pair, second_mask)
        volume_a = unembed(
            tokens_a, beside, unembed_weight[None], u_all, (1, 2), others[1:], me1, volume_a, e_pair, volume_b.shape, padded
        )
        e_rest = after(e_rest, volume_a)
        e_all = (e_pair, e_rest, flip(e_pair, core_mask), flip(e_rest, core_mask))
        tokens_b = embed(a.reshape(nv, tokens, padded), e_all, others, me1, sums, True, tokens_a.shape)
    else:
        every = jnp.arange(nv, dtype=jnp.int32)
        decode, encode = (
            lax.all_gather(w, "lat", axis=0, tiled=True).reshape(nv, rows, width)
            for w in (unembed_weight, embed_weight)
        )
        (a,) = im2col(volume_b, rim, edge, spread, dims, None, None, (edge, edge))
        volume_a = unembed(
            tokens_a, beside, decode, (), (None,) * nv, every, me1, None, edge, volume_b.shape, padded
        )
        tokens_b = embed(
            a.reshape(nv, tokens, padded), (encode,), every, me1, None, False, tokens_a.shape
        )
    return tokens_b, volume_a


def solution(mesh):
    placed = (
        P(None, None, "lat", "lon"),
        P(None, "lat", "lon", None),
        P("lat", None),
        P("lat", None),
    )
    return jax.shard_map(
        per_device,
        mesh=mesh,
        in_specs=placed,
        out_specs=(P(None, "lat", "lon", None), P(None, None, "lat", "lon")),
        check_vma=False,
    )
```

```python
import functools

import jax
import jax.numpy as jnp
import numpy as np
from jax import lax
from jax.experimental import pallas as pl
from jax.experimental.pallas import tpu as pltpu
from jax.sharding import PartitionSpec as P

BF = jnp.bfloat16
F32 = jnp.float32
VMEM_LIMIT = 56 * 1024 * 1024
SMALL_LIMIT = 36 * 1024 * 1024
DZ, DY, DX = 7, 12, 12
SK, SY, SX = 5, 8, 8
GROUP = 8


def params(limit=VMEM_LIMIT):
    return pltpu.CompilerParams(vmem_limit_bytes=limit)


def spread_matrix(nk, ni, nx):
    rows = np.arange(nk * nx)[:, None]
    cols = np.arange(DX * nk * ni)[None, :]
    dx, k, i = cols // (nk * ni), cols // ni % nk, cols % ni
    return ((rows // nx == k) & (rows % nx == SX * i - 2 + dx)).astype(BF)


def edge_lanes(nv, nk):
    lane = np.arange(4 * nv * nk)
    return lane // (2 * nv * nk), lane // (2 * nk) % nv, lane // nk % 2, lane % nk


def pick_matrix(nv, nk, nx):
    side, v, c, k = edge_lanes(nv, nk)
    rows = np.arange(nk * nx)[None, :, None]
    x = np.where(side == 0, nx - 2 + c, c)
    own = np.arange(nv)[:, None, None] == v
    return (own & (rows // nx == k) & (rows % nx == x)).astype(BF)


def edge_matrix(nv, nk, ni):
    side, v, c, k = (np.tile(a, 2)[None, :, None] for a in edge_lanes(nv, nk))
    half = (np.arange(8 * nv * nk) // (4 * nv * nk))[None, :, None]
    cols = np.arange(4 * nk * ni)[None, None, :]
    d, kk, i = cols // (nk * ni), cols // ni % nk, cols % ni
    own = np.arange(nv)[:, None, None] == v
    left = (half == 0) & (side == 0) & (i == 0) & (d == c)
    right = (half == 1) & (side == 1) & (i == ni - 1) & (d == 2 + c)
    return (own & (k == kk) & (left | right)).astype(BF)


def column_lanes(nk, nj):
    tall = nj + 2
    lanes = -(-2 * nk * tall // 128) * 128
    return tall, lanes


def decode_matrix(nk, nj, ni, nx):
    tall, lanes = column_lanes(nk, nj)
    rows = np.arange(nk * nx)[:, None]
    cols = np.arange(2 * lanes)[None, :]
    c, lane = cols // lanes, cols % lanes
    side, k = lane // (nk * tall), lane // tall % nk
    x = np.where(side == 0, c, nx - 2 + c)
    beside = (side < 2) & (rows // nx == k) & (rows % nx == x)
    return np.concatenate([spread_matrix(nk, ni, nx), beside.astype(BF)], axis=1)


def stack_levels(read, levels, nk, zeros, lhs, at, rows, dz):
    for k in range(nk):
        level = SK * k - 1 + dz
        block = read(level) if 0 <= level < levels else zeros
        lhs[at : at + rows, k * 128 : (k + 1) * 128] = block


def stack_rim(rim, levels, nk, lhs, main):
    none = jnp.zeros((8, rim.shape[3]), F32)
    for k in range(nk):
        blocks = []
        for dz in range(DZ + 1):
            level = SK * k - 1 + dz
            blocks.append(rim[0, level] if 0 <= level < levels and dz < DZ else none)
        lhs[main : main + 64, k * 128 : (k + 1) * 128] = jnp.concatenate(blocks, axis=0).astype(BF)


def pack_kernel(nk, vol, rim, pick, dep, out, lhs, acc):
    v = pl.program_id(0)
    _, levels, ny, nx = vol.shape
    for dz in range(DZ):
        stack_levels(lambda l: vol[0, l].astype(BF), levels, nk, jnp.zeros((ny, nx), BF), lhs, dz * ny, ny, dz)
    stack_rim(rim, levels, nk, lhs, DZ * ny)
    part = jnp.dot(lhs[...], pick[0], preferred_element_type=F32)

    @pl.when(v == 0)
    def _():
        acc[...] = part

    @pl.when(v > 0)
    def _():
        acc[...] += part

    @pl.when(v == pl.num_programs(0) - 1)
    def _():
        out[...] = acc[...].astype(BF)


def im2col_kernel(nk, ni, nj, shard, with_own, vol, rim, edge, spread, edge_hot, dep, dep2, *refs):
    if with_own:
        own, weight, out, sums, lhs, q, w_buf, w_sem = refs
    else:
        out, lhs, q = refs
    v = pl.program_id(0)
    if with_own:
        copies = weight_copies(False, (weight,), 0, 0, w_buf, w_sem)

        @pl.when(v == 0)
        def _():
            for c in copies:
                c.start()

    _, levels, ny, nx = vol.shape
    main = DZ * ny
    for dz in range(DZ):
        stack_levels(lambda l: vol[0, l].astype(BF), levels, nk, jnp.zeros((ny, nx), BF), lhs, dz * ny, ny, dz)
    stack_rim(rim, levels, nk, lhs, main)
    for pair in range(DX // 2):
        got = jnp.dot(lhs[...], spread[:, pair * 256 : (pair + 1) * 256], preferred_element_type=F32)
        if pair in (0, DX // 2 - 1):
            which = 0 if pair == 0 else 1
            got += jnp.dot(edge[...], edge_hot[0, :, which * 256 : (which + 1) * 256], preferred_element_type=F32)
        for h in range(2):
            dx = 2 * pair + h
            mine = got[:, h * 128 : (h + 1) * 128]
            for dz in range(DZ):
                q[dz, pl.ds(2 * DX + dx, ny, stride=DX), :] = mine[dz * ny : (dz + 1) * ny]
                at = main + 8 * dz
                q[dz, pl.ds(dx, 2, stride=DX), :] = mine[at : at + 2]
                q[dz, pl.ds(DX * (ny + 2) + dx, 2, stride=DX), :] = mine[at + 2 : at + 4]
    rows, padded, piece = shard
    head = piece * (GROUP - 1)
    per = SY * DX
    for j in range(nj):
        columns = jnp.concatenate([q[dz, per * j : per * j + DY * DX, :] for dz in range(DZ)], axis=0)
        gap = jnp.zeros((padded - rows, 128), F32)
        columns = jnp.concatenate([columns[:head], gap, columns[head:]], axis=0)
        out[0, j] = columns.T.astype(BF)
    if with_own:

        @pl.when(v == 0)
        def _():
            for c in copies:
                c.wait()

        @pl.when(v == own[0])
        def _():
            windows = out[0].reshape(nj * nk * ni, padded)
            sums[...] = jnp.dot(windows, w_buf[...], preferred_element_type=F32)


def weight_copies(gathered, sources, step, me, slot, sems):
    padded = slot.shape[0]
    piece = padded // GROUP
    if not gathered:
        (source,) = sources
        rows = source.shape[1]
        head = piece * (GROUP - 1)
        return [
            pltpu.make_async_copy(source.at[step, pl.ds(0, head)], slot.at[pl.ds(0, head)], sems.at[0]),
            pltpu.make_async_copy(source.at[step, pl.ds(rows - piece, piece)], slot.at[pl.ds(head, piece)], sems.at[1]),
        ]
    core = lax.rem(me, 2)
    a, b = 2 + 2 * core, 4 - 2 * core
    distances = ((0, a), (b, 6), (1, 1 + b), (1 + a, 7))
    copies = []
    for n, (source, pair) in enumerate(zip(sources, distances)):
        for h, distance in enumerate(pair):
            place = pl.multiple_of(lax.bitwise_xor(me, jnp.int32(distance)) * piece, piece)
            copies.append(
                pltpu.make_async_copy(source.at[h, step], slot.at[pl.ds(place, piece)], sems.at[2 * n + h])
            )
    return copies


def embed_kernel(n, gathered, first, vid, me, a, *refs):
    n_w = 4 if gathered else 1
    sources, refs = refs[:n_w], refs[n_w:]
    if not first:
        prev, refs = refs[0], refs[1:]
    out, a_buf, w_buf, acc, before, a_sem, w_sem, p_sem = refs

    def copies(s):
        slot = s % 2
        return [pltpu.make_async_copy(a.at[vid[s]], a_buf.at[slot], a_sem.at[slot])] + weight_copies(
            gathered, sources, s, me[0], w_buf.at[slot], w_sem.at[slot]
        )

    for c in copies(0):
        c.start()
    for s in range(n):
        for c in copies(s):
            c.wait()
        if s + 1 < n:
            for c in copies(s + 1):
                c.start()
        if s == max(n - 2, 0) and not first:
            extra = pltpu.make_async_copy(prev, before, p_sem)
            extra.start()
        got = jnp.dot(a_buf[s % 2], w_buf[s % 2], preferred_element_type=F32)
        if s > 0:
            got += acc[...]
        if s < n - 1:
            acc[...] = got
            continue
        if not first:
            extra.wait()
            got += before[...]
        nk, nj, ni, width = out.shape
        for j in range(nj):
            out[:, j] = got[j * nk * ni : (j + 1) * nk * ni].astype(BF).reshape(nk, ni, width)


def unembed_kernel(kinds, vid, me, tokens, above, below, left, right, hot_hbm, own, dep, *refs):
    gathered = any(kind is not None for kind in kinds)
    sources, refs = (refs[:4], refs[4:]) if gathered else ((), refs)
    if kinds[0] is not None:
        refs = refs[1:]
    vol, w_buf, t, t_side, r, q, qc, lhs, hot, w_sem, t_sem, hot_sem = refs
    s, n = pl.program_id(0), pl.num_programs(0)
    nk, nj, ni, width = tokens.shape
    _, levels, ny, nx = vol.shape
    per, over, block = SY * DX, (DY - SY) * DX, DY * DX
    padded = w_buf.shape[1]
    head, gap = padded // GROUP * (GROUP - 1), padded - DZ * block
    tall, c_lanes = column_lanes(nk, nj)
    half = nk * tall
    row = nk * ni
    c_at = (nj + 2) * row

    def copies(step, kind):
        slot = lax.rem(step, 2)
        if kind is None:
            return weight_copies(False, (own,), step, 0, w_buf.at[slot], w_sem.at[slot])
        return weight_copies(True, sources, kind + step, me[0], w_buf.at[slot], w_sem.at[slot])

    begin = None if kinds[0] is None else kinds[0]
    rest = None if kinds[-1] is None else kinds[-1] - len(kinds) + 1
    hot_copy = pltpu.make_async_copy(hot_hbm, hot, hot_sem)
    token_copies = [pltpu.make_async_copy(tokens.at[:, j], t.at[j], t_sem.at[j]) for j in range(nj)] + [
        pltpu.make_async_copy(above, t.at[nj], t_sem.at[nj]),
        pltpu.make_async_copy(below, t.at[nj + 1], t_sem.at[nj + 1]),
        pltpu.make_async_copy(left, t_side.at[pl.ds(0, half)], t_sem.at[nj + 2]),
        pltpu.make_async_copy(right, t_side.at[pl.ds(half, half)], t_sem.at[nj + 3]),
    ]

    @pl.when(s == 0)
    def _():
        for c in copies(s, begin) + token_copies:
            c.start()
        hot_copy.start()
        if c_lanes > 2 * half:
            t_side[2 * half :, :] = jnp.zeros((c_lanes - 2 * half, width), BF)

    @pl.when(s == 0)
    def _():
        for c in copies(s, begin) + token_copies:
            c.wait()

    @pl.when(s > 0)
    def _():
        for c in copies(s, rest):
            c.wait()

    @pl.when(s + 1 < n)
    def _():
        for c in copies(s + 1, rest):
            c.start()

    weight = w_buf[lax.rem(s, 2)]
    for ref, start, stop in ((t, 0, c_at), (t_side, c_at, c_at + c_lanes)):
        r[:, start:stop] = lax.dot_general(
            weight, ref[...].reshape(-1, width), (((1,), (1,)), ((), ())), preferred_element_type=F32
        )

    def rows_of(dz, at, start, stop, lanes=128):
        lo, hi = dz * block + start, dz * block + stop
        if hi <= head:
            return r[lo:hi, at : at + lanes]
        if lo >= head:
            return r[lo + gap : hi + gap, at : at + lanes]
        return jnp.concatenate([r[lo:head, at : at + lanes], r[head + gap : hi + gap, at : at + lanes]], axis=0)

    up, down = nj * row, (nj + 1) * row
    lane = lax.broadcasted_iota(jnp.int32, (8, c_lanes), 1)[:1]
    side, place = lane // half, lax.rem(lane, tall)
    edge2 = 2 * DX
    for dz in range(DZ):
        for j in range(nj + 1):
            at = per * j
            first, last = (edge2 if j == 0 else 0), (edge2 if j == nj else over)
            before = up if j == 0 else (j - 1) * row
            after = down if j == nj else j * row
            q[dz, at + first : at + last, :] = rows_of(dz, after, first, last) + rows_of(
                dz, before, per + first, per + last
            )
            qc[dz, at + first : at + last, :] = jnp.where(
                place == j + 1,
                rows_of(dz, c_at, first, last, c_lanes),
                jnp.where(place == j, rows_of(dz, c_at, per + first, per + last, c_lanes), 0.0),
            )
            if j < nj:
                q[dz, at + over : at + per, :] = rows_of(dz, after, over, per)
                qc[dz, at + over : at + per, :] = jnp.where(place == j + 1, rows_of(dz, c_at, over, per, c_lanes), 0.0)
    for dz in range(DZ):
        rows = slice(dz * ny, (dz + 1) * ny)
        for dx in range(DX):
            lhs[rows, dx * row : (dx + 1) * row] = q[dz, pl.ds(2 * DX + dx, ny, stride=DX), :].astype(BF)
        for c in range(2):
            far = qc[dz, pl.ds(2 * DX + DX - 2 + c, ny, stride=DX), :]
            near = qc[dz, pl.ds(2 * DX + c, ny, stride=DX), :]
            at = DX * row + c * c_lanes
            lhs[rows, at : at + c_lanes] = jnp.where(side == 0, far, near).astype(BF)

    @pl.when(s == 0)
    def _():
        hot_copy.wait()

    carry = None
    for pair in range(nk // 2):
        got = lax.dot_general(
            lhs[...], hot[pair * 256 : (pair + 1) * 256, :], (((1,), (1,)), ((), ())), preferred_element_type=F32
        )
        for h in range(2):
            k = 2 * pair + h
            mine = got[:, h * 128 : (h + 1) * 128]
            for dz in range(DZ):
                level = SK * k - 1 + dz
                here = mine[dz * ny : (dz + 1) * ny]
                if dz < DZ - SK and k > 0:
                    here = here + carry[dz]
                if 0 <= level < levels and (dz < SK or k == nk - 1):
                    vol[0, level] = here
            carry = [mine[dz * ny : (dz + 1) * ny] for dz in range(SK, DZ)]


def whole(shape):
    return pl.BlockSpec(shape, lambda *_: (0,) * len(shape))


def lead(shape):
    return pl.BlockSpec((1,) + tuple(shape[1:]), lambda v, *_: (v,) + (0,) * (len(shape) - 1))


ANY = pl.BlockSpec(memory_space=pl.ANY)


def cost(flops, bytes_accessed):
    return pl.CostEstimate(flops=int(flops), bytes_accessed=int(bytes_accessed), transcendentals=0)


def pack_edges(volume, rim, nk, dep):
    nv, levels, ny, nx = volume.shape
    pick = pick_matrix(nv, nk, nx)
    rows = DZ * ny + 64
    return pl.pallas_call(
        functools.partial(pack_kernel, nk),
        grid=(nv,),
        in_specs=[lead(volume.shape), lead(rim.shape), lead(pick.shape), ANY],
        out_specs=whole((rows, 128)),
        out_shape=jax.ShapeDtypeStruct((rows, 128), BF),
        scratch_shapes=[pltpu.VMEM((rows, nk * nx), BF), pltpu.VMEM((rows, 128), F32)],
        compiler_params=params(SMALL_LIMIT),
        cost_estimate=cost(2 * nv * DZ * ny * nk * nx * 256, volume.size * 4),
        name="pack_edges",
    )(volume, rim, pick, dep)


def im2col(volume, rim, edge, spread, dims, own, weight, dep):
    nk, nj, ni, padded = dims
    nv, levels, ny, nx = volume.shape
    hot = edge_matrix(nv, nk, ni)
    rows = DZ * ny + 64
    shape = (nv, nj, nk * ni, padded)
    width = None if weight is None else weight.shape[-1]
    with_own = weight is not None
    extra_specs, extra, extra_out, extra_scratch = [], [], [], []
    if with_own:
        extra_specs, extra = [pl.BlockSpec(memory_space=pltpu.SMEM), ANY], [own, weight]
        extra_out = [(nj * nk * ni, width)]
        extra_scratch = [pltpu.VMEM((padded, width), BF), pltpu.SemaphoreType.DMA((2,))]
    return pl.pallas_call(
        functools.partial(im2col_kernel, nk, ni, nj, (DZ * DY * DX, padded, padded // GROUP), with_own),
        grid=(nv,),
        in_specs=[lead(volume.shape), lead(rim.shape), whole(edge.shape), whole(spread.shape), lead(hot.shape), ANY, ANY]
        + extra_specs,
        out_specs=[lead(shape)] + [whole(x) for x in extra_out],
        out_shape=[jax.ShapeDtypeStruct(shape, BF)] + [jax.ShapeDtypeStruct(x, F32) for x in extra_out],
        scratch_shapes=[pltpu.VMEM((rows, nk * nx), BF), pltpu.VMEM((DZ, DX * (ny + 4), 128), F32)] + extra_scratch,
        compiler_params=params(SMALL_LIMIT),
        cost_estimate=cost(3 * nv * rows * nk * nx * DX * 128, volume.size * 4 + 2 * nv * nj * 128 * padded),
        name="im2col",
    )(volume, rim, edge, spread, hot, *dep, *extra)


def embed(a, weights, vid, me, prev, gathered, token_shape):
    n = vid.shape[0]
    nv, rows, padded = a.shape
    width = weights[0].shape[-1]
    first = prev is None
    smem = pl.BlockSpec(memory_space=pltpu.SMEM)
    return pl.pallas_call(
        functools.partial(embed_kernel, n, gathered, first),
        in_specs=[smem, smem, ANY] + [ANY] * (len(weights) + (not first)),
        out_specs=pl.BlockSpec(memory_space=pltpu.VMEM),
        out_shape=jax.ShapeDtypeStruct(token_shape, BF),
        scratch_shapes=[
            pltpu.VMEM((2, rows, padded), BF),
            pltpu.VMEM((2, padded, width), BF),
            pltpu.VMEM((rows, width), F32),
            pltpu.VMEM((8, 128) if first else (rows, width), F32),
            pltpu.SemaphoreType.DMA((2,)),
            pltpu.SemaphoreType.DMA((2, GROUP)),
            pltpu.SemaphoreType.DMA,
        ],
        compiler_params=params(),
        cost_estimate=cost(2 * n * rows * padded * width, 2 * n * padded * (rows + width) + 4 * rows * width),
        name="embed",
    )(vid, me, a, *weights, *([] if first else [prev]))


def unembed(tokens, beside, own, gathered, kinds, vid, me, prev, dep, volume_shape, padded):
    nk, nj, ni, width = tokens.shape
    nv, levels, ny, nx = volume_shape
    hot = decode_matrix(nk, nj, ni, nx)
    tall, c_lanes = column_lanes(nk, nj)
    before = () if prev is None else (prev,)
    n = len(kinds)
    count = (nj + 2) * nk * ni + c_lanes
    return pl.pallas_call(
        functools.partial(unembed_kernel, kinds),
        grid_spec=pltpu.PrefetchScalarGridSpec(
            num_scalar_prefetch=2,
            grid=(len(kinds),),
            in_specs=[ANY] * (4 + len(beside) + len(gathered) + len(before)),
            out_specs=pl.BlockSpec((1, levels, ny, nx), lambda s, vid, me: (vid[s], 0, 0, 0)),
            scratch_shapes=[
                pltpu.VMEM((2, padded, width), BF),
                pltpu.VMEM((nj + 2, nk, ni, width), BF),
                pltpu.VMEM((c_lanes, width), BF),
                pltpu.VMEM((padded, count), F32),
                pltpu.VMEM((DZ, DX * (ny + 4), nk * ni), F32),
                pltpu.VMEM((DZ, DX * (ny + 4), c_lanes), F32),
                pltpu.VMEM((DZ * ny, hot.shape[1]), BF),
                pltpu.VMEM(hot.shape, BF),
                pltpu.SemaphoreType.DMA((2, GROUP)),
                pltpu.SemaphoreType.DMA((nj + 4,)),
                pltpu.SemaphoreType.DMA,
            ],
        ),
        out_shape=jax.ShapeDtypeStruct(volume_shape, F32),
        input_output_aliases={} if prev is None else {len(beside) + 6 + len(gathered): 0},
        compiler_params=params(),
        cost_estimate=cost(1000, 1000) if n == 1 else cost(8 * n * padded * width * nj * 128, 2 * n * padded * width + 4 * n * levels * ny * nx),
        name="unembed",
    )(vid, me, tokens, *beside, hot, own, dep, *gathered, *before)


def both_ways(up_rows, down_rows, axis, wrap):
    size = lax.axis_size(axis)
    up = [(i, (i + 1) % size) for i in range(size if wrap else size - 1)]
    return lax.ppermute(up_rows, axis, up), lax.ppermute(down_rows, axis, [(j, i) for i, j in up])


def piece_rows(rows):
    return -(-rows // (16 * GROUP)) * 16


def after(x, *others):
    return lax.optimization_barrier((x,) + others)[0]


def own_piece(weight, me):
    rows, piece = weight.shape[0], piece_rows(weight.shape[0])
    return lax.dynamic_slice_in_dim(weight, jnp.minimum(me * piece, rows - piece), piece, 0)


def from_lat(piece):
    size = lax.axis_size("lat")
    got = [lax.ppermute(piece, "lat", [(i, (i + s) % size) for i in range(size)]) for s in range(1, size)]
    return got


def flip(x, mask):
    return lax.ppermute(x, "lon", [(i, i ^ mask(i)) for i in range(lax.axis_size("lon"))])


def first_mask(i):
    return 2 + 2 * (i & 1)


def second_mask(i):
    return 4 - 2 * (i & 1)


def core_mask(i):
    return 1


def per_device(volume_b, tokens_a, embed_weight, unembed_weight):
    nk, nj, ni, width = tokens_a.shape
    nv, levels, ny, nx = volume_b.shape
    rows = DZ * DY * DX
    padded = piece_rows(rows) * GROUP
    main = DZ * ny
    lat, lats = lax.axis_index("lat"), lax.axis_size("lat")
    me = lax.rem(lax.axis_index("lon"), GROUP).astype(jnp.int32)
    me1 = me.reshape(1)
    fast = embed_weight.shape[0] == rows and lax.axis_size("lon") % GROUP == 0
    spread = spread_matrix(nk, ni, nx)

    def voxels(at):
        return lax.optimization_barrier(volume_b[:, :, at : at + 2]).astype(BF).reshape(-1, nx)

    above, below = (x.reshape(nv, levels, 2, nx) for x in both_ways(voxels(ny - 2), voxels(0), "lat", False))
    rim = jnp.concatenate([above, below, jnp.zeros((nv, levels, 4, nx), BF)], axis=2).astype(F32)
    row_above, row_below = both_ways(tokens_a[:, nj - 1], tokens_a[:, 0], "lat", False)

    start = volume_b
    if fast:
        start = own_piece(unembed_weight, me)
        u_near = from_lat(start)
    packed = pack_edges(volume_b, rim, nk, start)
    edge = jnp.concatenate(both_ways(packed, packed, "lon", True), axis=1)

    def column(i):
        return jnp.concatenate([row_above[:, i][:, None], tokens_a[:, :, i], row_below[:, i][:, None]], axis=1)

    left, right = both_ways(column(ni - 1), column(0), "lon", True)
    beside = [row_above, row_below, left.reshape(-1, width), right.reshape(-1, width)]
    dims = (nk, nj, ni, padded)
    tokens = nj * nk * ni

    if fast:
        u_near = jnp.stack(u_near)
        u_pair = jnp.stack([u_near, after(flip(u_near, first_mask), row_above, row_below)])
        u_rest = flip(u_pair, second_mask)
        e_got = from_lat(after(own_piece(embed_weight, me), u_near))
        own = lat.astype(jnp.int32).reshape(1)
        others = lax.rem(lat - jnp.arange(1, lats, dtype=jnp.int32) + lats, lats).astype(jnp.int32)
        a, sums = im2col(volume_b, rim, edge, spread, dims, own, embed_weight[None], (u_pair, edge))
        u_rest = after(u_rest, sums)
        u_all = (u_pair, u_rest, flip(u_pair, core_mask), flip(u_rest, core_mask))
        first_two = jnp.concatenate([own, others[:1]])
        volume_a = unembed(
            tokens_a, beside, unembed_weight[None], (), (None,), own, me1, None, sums, volume_b.shape, padded
        )
        e_near = jnp.stack([after(x, volume_a) for x in e_got])
        e_far = flip(e_near, first_mask)
        volume_a = unembed(
            tokens_a, beside, unembed_weight[None], u_all, (0,), others[:1], me1, volume_a, e_near, volume_b.shape, padded
        )
        e_pair = jnp.stack([e_near, after(e_far, volume_a)])
        e_rest = flip(e_pair, second_mask)
        volume_a = unembed(
            tokens_a, beside, unembed_weight[None], u_all, (1, 2), others[1:], me1, volume_a, e_pair, volume_b.shape, padded
        )
        e_rest = after(e_rest, volume_a)
        e_all = (e_pair, e_rest, flip(e_pair, core_mask), flip(e_rest, core_mask))
        tokens_b = embed(a.reshape(nv, tokens, padded), e_all, others, me1, sums, True, tokens_a.shape)
    else:
        every = jnp.arange(nv, dtype=jnp.int32)
        decode, encode = (
            lax.all_gather(w, "lat", axis=0, tiled=True).reshape(nv, rows, width)
            for w in (unembed_weight, embed_weight)
        )
        (a,) = im2col(volume_b, rim, edge, spread, dims, None, None, (edge, edge))
        volume_a = unembed(
            tokens_a, beside, decode, (), (None,) * nv, every, me1, None, edge, volume_b.shape, padded
        )
        tokens_b = embed(
            a.reshape(nv, tokens, padded), (encode,), every, me1, None, False, tokens_a.shape
        )
    return tokens_b, volume_a


def solution(mesh):
    placed = (
        P(None, None, "lat", "lon"),
        P(None, "lat", "lon", None),
        P("lat", None),
        P("lat", None),
    )
    return jax.shard_map(
        per_device,
        mesh=mesh,
        in_specs=placed,
        out_specs=(P(None, "lat", "lon", None), P(None, None, "lat", "lon")),
        check_vma=False,
    )
```

```python
import functools

import jax
import jax.numpy as jnp
import numpy as np
from jax import lax
from jax.experimental import pallas as pl
from jax.experimental.pallas import tpu as pltpu
from jax.sharding import PartitionSpec as P

BF = jnp.bfloat16
F32 = jnp.float32
VMEM_LIMIT = 56 * 1024 * 1024
SMALL_LIMIT = 36 * 1024 * 1024
DZ, DY, DX = 7, 12, 12
SK, SY, SX = 5, 8, 8
GROUP = 8


def params(limit=VMEM_LIMIT):
    return pltpu.CompilerParams(vmem_limit_bytes=limit)


def spread_matrix(nk, ni, nx):
    rows = np.arange(nk * nx)[:, None]
    cols = np.arange(DX * nk * ni)[None, :]
    dx, k, i = cols // (nk * ni), cols // ni % nk, cols % ni
    return ((rows // nx == k) & (rows % nx == SX * i - 2 + dx)).astype(BF)


def edge_lanes(nv, nk):
    lane = np.arange(4 * nv * nk)
    return lane // (2 * nv * nk), lane // (2 * nk) % nv, lane // nk % 2, lane % nk


def pick_matrix(nv, nk, nx):
    side, v, c, k = edge_lanes(nv, nk)
    rows = np.arange(nk * nx)[None, :, None]
    x = np.where(side == 0, nx - 2 + c, c)
    own = np.arange(nv)[:, None, None] == v
    return (own & (rows // nx == k) & (rows % nx == x)).astype(BF)


def edge_matrix(nv, nk, ni):
    side, v, c, k = (np.tile(a, 2)[None, :, None] for a in edge_lanes(nv, nk))
    half = (np.arange(8 * nv * nk) // (4 * nv * nk))[None, :, None]
    cols = np.arange(4 * nk * ni)[None, None, :]
    d, kk, i = cols // (nk * ni), cols // ni % nk, cols % ni
    own = np.arange(nv)[:, None, None] == v
    left = (half == 0) & (side == 0) & (i == 0) & (d == c)
    right = (half == 1) & (side == 1) & (i == ni - 1) & (d == 2 + c)
    return (own & (k == kk) & (left | right)).astype(BF)


def column_lanes(nk, nj):
    tall = nj + 2
    lanes = -(-2 * nk * tall // 128) * 128
    return tall, lanes


def decode_matrix(nk, nj, ni, nx):
    tall, lanes = column_lanes(nk, nj)
    rows = np.arange(nk * nx)[:, None]
    cols = np.arange(2 * lanes)[None, :]
    c, lane = cols // lanes, cols % lanes
    side, k = lane // (nk * tall), lane // tall % nk
    x = np.where(side == 0, c, nx - 2 + c)
    beside = (side < 2) & (rows // nx == k) & (rows % nx == x)
    return np.concatenate([spread_matrix(nk, ni, nx), beside.astype(BF)], axis=1)


def stack_levels(read, levels, nk, zeros, lhs, at, rows, dz):
    for k in range(nk):
        level = SK * k - 1 + dz
        block = read(level) if 0 <= level < levels else zeros
        lhs[at : at + rows, k * 128 : (k + 1) * 128] = block


def stack_rim(rim, levels, nk, lhs, main):
    none = jnp.zeros((8, rim.shape[3]), F32)
    for k in range(nk):
        blocks = []
        for dz in range(DZ + 1):
            level = SK * k - 1 + dz
            blocks.append(rim[0, level] if 0 <= level < levels and dz < DZ else none)
        lhs[main : main + 64, k * 128 : (k + 1) * 128] = jnp.concatenate(blocks, axis=0).astype(BF)


def pack_kernel(nk, vol, rim, pick, dep, out, lhs, acc):
    v = pl.program_id(0)
    _, levels, ny, nx = vol.shape
    for dz in range(DZ):
        stack_levels(lambda l: vol[0, l].astype(BF), levels, nk, jnp.zeros((ny, nx), BF), lhs, dz * ny, ny, dz)
    stack_rim(rim, levels, nk, lhs, DZ * ny)
    part = jnp.dot(lhs[...], pick[0], preferred_element_type=F32)

    @pl.when(v == 0)
    def _():
        acc[...] = part

    @pl.when(v > 0)
    def _():
        acc[...] += part

    @pl.when(v == pl.num_programs(0) - 1)
    def _():
        out[...] = acc[...].astype(BF)


def im2col_kernel(nk, ni, nj, shard, with_own, vol, rim, edge, spread, edge_hot, dep, dep2, *refs):
    if with_own:
        own, weight, out, sums, lhs, q, w_buf, w_sem = refs
    else:
        out, lhs, q = refs
    v = pl.program_id(0)
    if with_own:
        copies = weight_copies(False, (weight,), 0, 0, w_buf, w_sem)

        @pl.when(v == 0)
        def _():
            for c in copies:
                c.start()

    _, levels, ny, nx = vol.shape
    main = DZ * ny
    for dz in range(DZ):
        stack_levels(lambda l: vol[0, l].astype(BF), levels, nk, jnp.zeros((ny, nx), BF), lhs, dz * ny, ny, dz)
    stack_rim(rim, levels, nk, lhs, main)
    for pair in range(DX // 2):
        got = jnp.dot(lhs[...], spread[:, pair * 256 : (pair + 1) * 256], preferred_element_type=F32)
        if pair in (0, DX // 2 - 1):
            which = 0 if pair == 0 else 1
            got += jnp.dot(edge[...], edge_hot[0, :, which * 256 : (which + 1) * 256], preferred_element_type=F32)
        for h in range(2):
            dx = 2 * pair + h
            mine = got[:, h * 128 : (h + 1) * 128]
            for dz in range(DZ):
                q[dz, pl.ds(2 * DX + dx, ny, stride=DX), :] = mine[dz * ny : (dz + 1) * ny]
                at = main + 8 * dz
                q[dz, pl.ds(dx, 2, stride=DX), :] = mine[at : at + 2]
                q[dz, pl.ds(DX * (ny + 2) + dx, 2, stride=DX), :] = mine[at + 2 : at + 4]
    rows, padded, piece = shard
    head = piece * (GROUP - 1)
    per = SY * DX
    for j in range(nj):
        columns = jnp.concatenate([q[dz, per * j : per * j + DY * DX, :] for dz in range(DZ)], axis=0)
        gap = jnp.zeros((padded - rows, 128), F32)
        columns = jnp.concatenate([columns[:head], gap, columns[head:]], axis=0)
        out[0, j] = columns.T.astype(BF)
    if with_own:

        @pl.when(v == 0)
        def _():
            for c in copies:
                c.wait()

        @pl.when(v == own[0])
        def _():
            windows = out[0].reshape(nj * nk * ni, padded)
            sums[...] = jnp.dot(windows, w_buf[...], preferred_element_type=F32)


def weight_copies(gathered, sources, step, me, slot, sems):
    padded = slot.shape[0]
    piece = padded // GROUP
    if not gathered:
        (source,) = sources
        rows = source.shape[1]
        head = piece * (GROUP - 1)
        return [
            pltpu.make_async_copy(source.at[step, pl.ds(0, head)], slot.at[pl.ds(0, head)], sems.at[0]),
            pltpu.make_async_copy(source.at[step, pl.ds(rows - piece, piece)], slot.at[pl.ds(head, piece)], sems.at[1]),
        ]
    core = lax.rem(me, 2)
    a, b = 2 + 2 * core, 4 - 2 * core
    distances = ((0, a), (b, 6), (1, 1 + b), (1 + a, 7))
    copies = []
    for n, (source, pair) in enumerate(zip(sources, distances)):
        for h, distance in enumerate(pair):
            place = pl.multiple_of(lax.bitwise_xor(me, jnp.int32(distance)) * piece, piece)
            copies.append(
                pltpu.make_async_copy(source.at[h, step], slot.at[pl.ds(place, piece)], sems.at[2 * n + h])
            )
    return copies


def embed_kernel(n, gathered, first, vid, me, a, *refs):
    n_w = 4 if gathered else 1
    sources, refs = refs[:n_w], refs[n_w:]
    if not first:
        prev, refs = refs[0], refs[1:]
    out, a_buf, w_buf, acc, before, a_sem, w_sem, p_sem = refs

    def copies(s):
        slot = s % 2
        return [pltpu.make_async_copy(a.at[vid[s]], a_buf.at[slot], a_sem.at[slot])] + weight_copies(
            gathered, sources, s, me[0], w_buf.at[slot], w_sem.at[slot]
        )

    for c in copies(0):
        c.start()
    for s in range(n):
        for c in copies(s):
            c.wait()
        if s + 1 < n:
            for c in copies(s + 1):
                c.start()
        if s == max(n - 2, 0) and not first:
            extra = pltpu.make_async_copy(prev, before, p_sem)
            extra.start()
        got = jnp.dot(a_buf[s % 2], w_buf[s % 2], preferred_element_type=F32)
        if s > 0:
            got += acc[...]
        if s < n - 1:
            acc[...] = got
            continue
        if not first:
            extra.wait()
            got += before[...]
        nk, nj, ni, width = out.shape
        for j in range(nj):
            out[:, j] = got[j * nk * ni : (j + 1) * nk * ni].astype(BF).reshape(nk, ni, width)


def unembed_kernel(kinds, vid, me, tokens, above, below, left, right, hot_hbm, own, dep, *refs):
    gathered = any(kind is not None for kind in kinds)
    sources, refs = (refs[:4], refs[4:]) if gathered else ((), refs)
    if kinds[0] is not None:
        refs = refs[1:]
    vol, w_buf, t, t_side, r, q, qc, lhs, hot, w_sem, t_sem, hot_sem = refs
    s, n = pl.program_id(0), pl.num_programs(0)
    nk, nj, ni, width = tokens.shape
    _, levels, ny, nx = vol.shape
    per, over, block = SY * DX, (DY - SY) * DX, DY * DX
    padded = w_buf.shape[1]
    head, gap = padded // GROUP * (GROUP - 1), padded - DZ * block
    tall, c_lanes = column_lanes(nk, nj)
    half = nk * tall
    row = nk * ni
    c_at = (nj + 2) * row

    def copies(step, kind):
        slot = lax.rem(step, 2)
        if kind is None:
            return weight_copies(False, (own,), step, 0, w_buf.at[slot], w_sem.at[slot])
        return weight_copies(True, sources, kind + step, me[0], w_buf.at[slot], w_sem.at[slot])

    begin = None if kinds[0] is None else kinds[0]
    rest = None if kinds[-1] is None else kinds[-1] - len(kinds) + 1
    hot_copy = pltpu.make_async_copy(hot_hbm, hot, hot_sem)
    token_copies = [pltpu.make_async_copy(tokens.at[:, j], t.at[j], t_sem.at[j]) for j in range(nj)] + [
        pltpu.make_async_copy(above, t.at[nj], t_sem.at[nj]),
        pltpu.make_async_copy(below, t.at[nj + 1], t_sem.at[nj + 1]),
        pltpu.make_async_copy(left, t_side.at[pl.ds(0, half)], t_sem.at[nj + 2]),
        pltpu.make_async_copy(right, t_side.at[pl.ds(half, half)], t_sem.at[nj + 3]),
    ]

    @pl.when(s == 0)
    def _():
        for c in copies(s, begin) + token_copies:
            c.start()
        if c_lanes > 2 * half:
            t_side[2 * half :, :] = jnp.zeros((c_lanes - 2 * half, width), BF)

    @pl.when(s == 0)
    def _():
        for c in copies(s, begin) + token_copies:
            c.wait()
        hot_copy.start()

    @pl.when(s > 0)
    def _():
        for c in copies(s, rest):
            c.wait()

    @pl.when(s + 1 < n)
    def _():
        for c in copies(s + 1, rest):
            c.start()

    weight = w_buf[lax.rem(s, 2)]
    for ref, start, stop in ((t, 0, c_at), (t_side, c_at, c_at + c_lanes)):
        r[:, start:stop] = lax.dot_general(
            weight, ref[...].reshape(-1, width), (((1,), (1,)), ((), ())), preferred_element_type=F32
        )

    def rows_of(dz, at, start, stop, lanes=128):
        lo, hi = dz * block + start, dz * block + stop
        if hi <= head:
            return r[lo:hi, at : at + lanes]
        if lo >= head:
            return r[lo + gap : hi + gap, at : at + lanes]
        return jnp.concatenate([r[lo:head, at : at + lanes], r[head + gap : hi + gap, at : at + lanes]], axis=0)

    up, down = nj * row, (nj + 1) * row
    lane = lax.broadcasted_iota(jnp.int32, (8, c_lanes), 1)[:1]
    side, place = lane // half, lax.rem(lane, tall)
    edge2 = 2 * DX
    for dz in range(DZ):
        for j in range(nj + 1):
            at = per * j
            first, last = (edge2 if j == 0 else 0), (edge2 if j == nj else over)
            before = up if j == 0 else (j - 1) * row
            after = down if j == nj else j * row
            q[dz, at + first : at + last, :] = rows_of(dz, after, first, last) + rows_of(
                dz, before, per + first, per + last
            )
            qc[dz, at + first : at + last, :] = jnp.where(
                place == j + 1,
                rows_of(dz, c_at, first, last, c_lanes),
                jnp.where(place == j, rows_of(dz, c_at, per + first, per + last, c_lanes), 0.0),
            )
            if j < nj:
                q[dz, at + over : at + per, :] = rows_of(dz, after, over, per)
                qc[dz, at + over : at + per, :] = jnp.where(place == j + 1, rows_of(dz, c_at, over, per, c_lanes), 0.0)
    for dz in range(DZ):
        rows = slice(dz * ny, (dz + 1) * ny)
        for dx in range(DX):
            lhs[rows, dx * row : (dx + 1) * row] = q[dz, pl.ds(2 * DX + dx, ny, stride=DX), :].astype(BF)
        for c in range(2):
            far = qc[dz, pl.ds(2 * DX + DX - 2 + c, ny, stride=DX), :]
            near = qc[dz, pl.ds(2 * DX + c, ny, stride=DX), :]
            at = DX * row + c * c_lanes
            lhs[rows, at : at + c_lanes] = jnp.where(side == 0, far, near).astype(BF)

    @pl.when(s == 0)
    def _():
        hot_copy.wait()

    carry = None
    for pair in range(nk // 2):
        got = lax.dot_general(
            lhs[...], hot[pair * 256 : (pair + 1) * 256, :], (((1,), (1,)), ((), ())), preferred_element_type=F32
        )
        for h in range(2):
            k = 2 * pair + h
            mine = got[:, h * 128 : (h + 1) * 128]
            for dz in range(DZ):
                level = SK * k - 1 + dz
                here = mine[dz * ny : (dz + 1) * ny]
                if dz < DZ - SK and k > 0:
                    here = here + carry[dz]
                if 0 <= level < levels and (dz < SK or k == nk - 1):
                    vol[0, level] = here
            carry = [mine[dz * ny : (dz + 1) * ny] for dz in range(SK, DZ)]


def whole(shape):
    return pl.BlockSpec(shape, lambda *_: (0,) * len(shape))


def lead(shape):
    return pl.BlockSpec((1,) + tuple(shape[1:]), lambda v, *_: (v,) + (0,) * (len(shape) - 1))


ANY = pl.BlockSpec(memory_space=pl.ANY)


def cost(flops, bytes_accessed):
    return pl.CostEstimate(flops=int(flops), bytes_accessed=int(bytes_accessed), transcendentals=0)


def pack_edges(volume, rim, nk, dep):
    nv, levels, ny, nx = volume.shape
    pick = pick_matrix(nv, nk, nx)
    rows = DZ * ny + 64
    return pl.pallas_call(
        functools.partial(pack_kernel, nk),
        grid=(nv,),
        in_specs=[lead(volume.shape), lead(rim.shape), lead(pick.shape), ANY],
        out_specs=whole((rows, 128)),
        out_shape=jax.ShapeDtypeStruct((rows, 128), BF),
        scratch_shapes=[pltpu.VMEM((rows, nk * nx), BF), pltpu.VMEM((rows, 128), F32)],
        compiler_params=params(SMALL_LIMIT),
        cost_estimate=cost(2 * nv * DZ * ny * nk * nx * 256, volume.size * 4),
        name="pack_edges",
    )(volume, rim, pick, dep)


def im2col(volume, rim, edge, spread, dims, own, weight, dep):
    nk, nj, ni, padded = dims
    nv, levels, ny, nx = volume.shape
    hot = edge_matrix(nv, nk, ni)
    rows = DZ * ny + 64
    shape = (nv, nj, nk * ni, padded)
    width = None if weight is None else weight.shape[-1]
    with_own = weight is not None
    extra_specs, extra, extra_out, extra_scratch = [], [], [], []
    if with_own:
        extra_specs, extra = [pl.BlockSpec(memory_space=pltpu.SMEM), ANY], [own, weight]
        extra_out = [(nj * nk * ni, width)]
        extra_scratch = [pltpu.VMEM((padded, width), BF), pltpu.SemaphoreType.DMA((2,))]
    return pl.pallas_call(
        functools.partial(im2col_kernel, nk, ni, nj, (DZ * DY * DX, padded, padded // GROUP), with_own),
        grid=(nv,),
        in_specs=[lead(volume.shape), lead(rim.shape), whole(edge.shape), whole(spread.shape), lead(hot.shape), ANY, ANY]
        + extra_specs,
        out_specs=[lead(shape)] + [whole(x) for x in extra_out],
        out_shape=[jax.ShapeDtypeStruct(shape, BF)] + [jax.ShapeDtypeStruct(x, F32) for x in extra_out],
        scratch_shapes=[pltpu.VMEM((rows, nk * nx), BF), pltpu.VMEM((DZ, DX * (ny + 4), 128), F32)] + extra_scratch,
        compiler_params=params(SMALL_LIMIT),
        cost_estimate=cost(3 * nv * rows * nk * nx * DX * 128, volume.size * 4 + 2 * nv * nj * 128 * padded),
        name="im2col",
    )(volume, rim, edge, spread, hot, *dep, *extra)


def embed(a, weights, vid, me, prev, gathered, token_shape):
    n = vid.shape[0]
    nv, rows, padded = a.shape
    width = weights[0].shape[-1]
    first = prev is None
    smem = pl.BlockSpec(memory_space=pltpu.SMEM)
    return pl.pallas_call(
        functools.partial(embed_kernel, n, gathered, first),
        in_specs=[smem, smem, ANY] + [ANY] * (len(weights) + (not first)),
        out_specs=pl.BlockSpec(memory_space=pltpu.VMEM),
        out_shape=jax.ShapeDtypeStruct(token_shape, BF),
        scratch_shapes=[
            pltpu.VMEM((2, rows, padded), BF),
            pltpu.VMEM((2, padded, width), BF),
            pltpu.VMEM((rows, width), F32),
            pltpu.VMEM((8, 128) if first else (rows, width), F32),
            pltpu.SemaphoreType.DMA((2,)),
            pltpu.SemaphoreType.DMA((2, GROUP)),
            pltpu.SemaphoreType.DMA,
        ],
        compiler_params=params(),
        cost_estimate=cost(2 * n * rows * padded * width, 2 * n * padded * (rows + width) + 4 * rows * width),
        name="embed",
    )(vid, me, a, *weights, *([] if first else [prev]))


def unembed(tokens, beside, own, gathered, kinds, vid, me, prev, dep, volume_shape, padded):
    nk, nj, ni, width = tokens.shape
    nv, levels, ny, nx = volume_shape
    hot = decode_matrix(nk, nj, ni, nx)
    tall, c_lanes = column_lanes(nk, nj)
    before = () if prev is None else (prev,)
    n = len(kinds)
    count = (nj + 2) * nk * ni + c_lanes
    return pl.pallas_call(
        functools.partial(unembed_kernel, kinds),
        grid_spec=pltpu.PrefetchScalarGridSpec(
            num_scalar_prefetch=2,
            grid=(len(kinds),),
            in_specs=[ANY] * (4 + len(beside) + len(gathered) + len(before)),
            out_specs=pl.BlockSpec((1, levels, ny, nx), lambda s, vid, me: (vid[s], 0, 0, 0)),
            scratch_shapes=[
                pltpu.VMEM((2, padded, width), BF),
                pltpu.VMEM((nj + 2, nk, ni, width), BF),
                pltpu.VMEM((c_lanes, width), BF),
                pltpu.VMEM((padded, count), F32),
                pltpu.VMEM((DZ, DX * (ny + 4), nk * ni), F32),
                pltpu.VMEM((DZ, DX * (ny + 4), c_lanes), F32),
                pltpu.VMEM((DZ * ny, hot.shape[1]), BF),
                pltpu.VMEM(hot.shape, BF),
                pltpu.SemaphoreType.DMA((2, GROUP)),
                pltpu.SemaphoreType.DMA((nj + 4,)),
                pltpu.SemaphoreType.DMA,
            ],
        ),
        out_shape=jax.ShapeDtypeStruct(volume_shape, F32),
        input_output_aliases={} if prev is None else {len(beside) + 6 + len(gathered): 0},
        compiler_params=params(),
        cost_estimate=cost(1000, 1000) if n == 1 else cost(8 * n * padded * width * nj * 128, 2 * n * padded * width + 4 * n * levels * ny * nx),
        name="unembed",
    )(vid, me, tokens, *beside, hot, own, dep, *gathered, *before)


def both_ways(up_rows, down_rows, axis, wrap):
    size = lax.axis_size(axis)
    up = [(i, (i + 1) % size) for i in range(size if wrap else size - 1)]
    return lax.ppermute(up_rows, axis, up), lax.ppermute(down_rows, axis, [(j, i) for i, j in up])


def piece_rows(rows):
    return -(-rows // (16 * GROUP)) * 16


def after(x, *others):
    return lax.optimization_barrier((x,) + others)[0]


def own_piece(weight, me):
    rows, piece = weight.shape[0], piece_rows(weight.shape[0])
    return lax.dynamic_slice_in_dim(weight, jnp.minimum(me * piece, rows - piece), piece, 0)


def from_lat(piece):
    size = lax.axis_size("lat")
    got = [lax.ppermute(piece, "lat", [(i, (i + s) % size) for i in range(size)]) for s in range(1, size)]
    return got


def flip(x, mask):
    return lax.ppermute(x, "lon", [(i, i ^ mask(i)) for i in range(lax.axis_size("lon"))])


def first_mask(i):
    return 2 + 2 * (i & 1)


def second_mask(i):
    return 4 - 2 * (i & 1)


def core_mask(i):
    return 1


def per_device(volume_b, tokens_a, embed_weight, unembed_weight):
    nk, nj, ni, width = tokens_a.shape
    nv, levels, ny, nx = volume_b.shape
    rows = DZ * DY * DX
    padded = piece_rows(rows) * GROUP
    main = DZ * ny
    lat, lats = lax.axis_index("lat"), lax.axis_size("lat")
    me = lax.rem(lax.axis_index("lon"), GROUP).astype(jnp.int32)
    me1 = me.reshape(1)
    fast = embed_weight.shape[0] == rows and lax.axis_size("lon") % GROUP == 0
    spread = spread_matrix(nk, ni, nx)

    def voxels(at):
        return lax.optimization_barrier(volume_b[:, :, at : at + 2]).astype(BF).reshape(-1, nx)

    above, below = (x.reshape(nv, levels, 2, nx) for x in both_ways(voxels(ny - 2), voxels(0), "lat", False))
    rim = jnp.concatenate([above, below, jnp.zeros((nv, levels, 4, nx), BF)], axis=2).astype(F32)
    row_above, row_below = both_ways(tokens_a[:, nj - 1], tokens_a[:, 0], "lat", False)

    start = volume_b
    if fast:
        start = own_piece(unembed_weight, me)
        u_near = from_lat(start)
    packed = pack_edges(volume_b, rim, nk, start)
    edge = jnp.concatenate(both_ways(packed, packed, "lon", True), axis=1)

    def column(i):
        return jnp.concatenate([row_above[:, i][:, None], tokens_a[:, :, i], row_below[:, i][:, None]], axis=1)

    left, right = both_ways(column(ni - 1), column(0), "lon", True)
    beside = [row_above, row_below, left.reshape(-1, width), right.reshape(-1, width)]
    dims = (nk, nj, ni, padded)
    tokens = nj * nk * ni

    if fast:
        u_near = jnp.stack(u_near)
        e_own = own_piece(embed_weight, me)
        u_pair = jnp.stack([u_near, after(flip(u_near, first_mask), row_above, row_below)])
        u_rest = flip(u_pair, second_mask)
        e_got = from_lat(after(e_own, u_near))
        own = lat.astype(jnp.int32).reshape(1)
        others = lax.rem(lat - jnp.arange(1, lats, dtype=jnp.int32) + lats, lats).astype(jnp.int32)
        a, sums = im2col(volume_b, rim, edge, spread, dims, own, embed_weight[None], (u_pair, after(edge, e_own)))
        u_rest = after(u_rest, sums)
        u_all = (u_pair, u_rest, flip(u_pair, core_mask), flip(u_rest, core_mask))
        first_two = jnp.concatenate([own, others[:1]])
        volume_a = unembed(
            tokens_a, beside, unembed_weight[None], (), (None,), own, me1, None, sums, volume_b.shape, padded
        )
        e_near = jnp.stack([after(x, volume_a) for x in e_got])
        e_far = flip(e_near, first_mask)
        volume_a = unembed(
            tokens_a, beside, unembed_weight[None], u_all, (0,), others[:1], me1, volume_a, e_near, volume_b.shape, padded
        )
        e_pair = jnp.stack([e_near, after(e_far, volume_a)])
        e_rest = flip(e_pair, second_mask)
        volume_a = unembed(
            tokens_a, beside, unembed_weight[None], u_all, (1, 2), others[1:], me1, volume_a, e_pair, volume_b.shape, padded
        )
        e_rest = after(e_rest, volume_a)
        e_all = (e_pair, e_rest, flip(e_pair, core_mask), flip(e_rest, core_mask))
        tokens_b = embed(a.reshape(nv, tokens, padded), e_all, others, me1, sums, True, tokens_a.shape)
    else:
        every = jnp.arange(nv, dtype=jnp.int32)
        decode, encode = (
            lax.all_gather(w, "lat", axis=0, tiled=True).reshape(nv, rows, width)
            for w in (unembed_weight, embed_weight)
        )
        (a,) = im2col(volume_b, rim, edge, spread, dims, None, None, (edge, edge))
        volume_a = unembed(
            tokens_a, beside, decode, (), (None,) * nv, every, me1, None, edge, volume_b.shape, padded
        )
        tokens_b = embed(
            a.reshape(nv, tokens, padded), (encode,), every, me1, None, False, tokens_a.shape
        )
    return tokens_b, volume_a


def solution(mesh):
    placed = (
        P(None, None, "lat", "lon"),
        P(None, "lat", "lon", None),
        P("lat", None),
        P("lat", None),
    )
    return jax.shard_map(
        per_device,
        mesh=mesh,
        in_specs=placed,
        out_specs=(P(None, "lat", "lon", None), P(None, None, "lat", "lon")),
        check_vma=False,
    )
```
